512 devices in a mesh: dp: 128 (over x, z, y_hi), mp: 4 (over y_lo, core).
Axes of the slice: x: 4, y: 4 (y_hi: 2, y_lo: 2; y = y_hi * 2 + y_lo), z: 16, core: 2. Of those that a mesh axis runs over, the one named last changes fastest.
Arguments:
- picture_encoder_outputs: bfloat16 [24576, 1536], P('dp', 'mp'), may hold values from -100 to 100
- caption_encoder_outputs: bfloat16 [24576, 1536], P('dp', 'mp'), may hold values from -100 to 100
- picture_mapping_matrix: bfloat16 [1536, 1536], P('mp'), may hold values from -0.15625 to 0.15625
- caption_mapping_matrix: bfloat16 [1536, 1536], P('mp'), may hold values from -0.15625 to 0.15625
- scale_exponent_param: float32 [1], replicated, may hold values from 3 to 4
- score_shift_param: float32 [1], replicated, may hold values from -3 to -1
- partner_caption_row: int32 [128, 192], P('dp'), may hold values from 0 to 191, each once within a row
Outputs:
- img_grad: bfloat16 [24576, 1536], P('dp', 'mp')
- txt_grad: bfloat16 [24576, 1536], P('dp', 'mp')
- row_loss: float32 [24576], P('dp')
The draws below stay inside these ranges and needn't reach their ends.
Inputs may be any that keep to these rules, and one draw needn't show every extreme that they name: `partner_caption_row`: each row of 192 entries names every row of its block once.
All inputs are finite; a program needn't handle non-finite values.
Results may differ from the reference program's by a relative error of at most 0.018.
Values may be sent and summed in bfloat16 or wider, within the bound.
A program may use at most 64 MiB of HBM per device.

```python
import math
import jax
import jax.numpy as jnp
from jax import lax

F = 1536
E = 1536
B_DEV = 192
STEPS = 8
SPANS = 128
TOKENS = 24576


def scaled_features(key):
    row_key, col_key, normal_key = jax.random.split(key, 3)
    row_scale = jnp.exp(jax.random.uniform(row_key, (TOKENS, 1), jnp.float32, 0.0, math.log(10.0)))
    col_scale = jnp.exp(jax.random.uniform(col_key, (1, F), jnp.float32, math.log(0.5), math.log(2.0)))
    normal_part = jnp.clip(jax.random.normal(normal_key, (TOKENS, F), jnp.float32), -4.0, 4.0)
    mixed = normal_part
    return (mixed * row_scale * col_scale).astype(jnp.bfloat16)


def draw_picture_encoder_outputs(key, part):
    key = jax.random.fold_in(key, 11)
    return scaled_features(key)


def draw_caption_encoder_outputs(key, part):
    key = jax.random.fold_in(key, 23)
    return scaled_features(key)


def block_scale(stream_key, dims, cuts, smallest, top_value):
    def one(position, shards_of):
        steps = jax.random.uniform(jax.random.fold_in(jax.random.fold_in(stream_key, 6), position), (shards_of,), jnp.float32, smallest / len(cuts), top_value / len(cuts))
        return jnp.repeat(jnp.exp(steps), dims[position] // shards_of).reshape((-1,) + (1,) * (len(dims) - position - 1))

    gain = one(*cuts[0])
    for cut in cuts[1:]:
        gain = gain * one(*cut)
    return gain


def scatter_about(rng, dims, width, limit, cuts=(), kind=jnp.bfloat16):
    values = width * jax.random.normal(rng, dims, jnp.float32)
    if cuts:
        values = values * block_scale(rng, dims, cuts, -0.22, 0.18)
    return jnp.clip(values, -limit, limit).astype(kind)


def setup_inputs(seed: int = 0) -> dict:
    splits = jax.random.split(jax.random.key(seed), 8)
    return {
        "picture_encoder_outputs": draw_picture_encoder_outputs(jax.random.fold_in(splits[7], 71), 0),
        "caption_encoder_outputs": draw_caption_encoder_outputs(jax.random.fold_in(splits[7], 71), 0),
        "picture_mapping_matrix": scatter_about(splits[2], (F, E), F ** -0.5, 0.15625, ((0, 4),)),
        "caption_mapping_matrix": scatter_about(splits[3], (F, E), F ** -0.5, 0.15625, ((0, 4),)),
        "scale_exponent_param": jnp.clip(jax.random.uniform(splits[4], (1,), jnp.float32, 3.0, 4.0), 3.0, 4.0),
        "score_shift_param": jnp.clip(jax.random.uniform(splits[5], (1,), jnp.float32, -3.0, -1.0), -3.0, -1.0),
        "partner_caption_row": jax.vmap(lambda own: jax.random.permutation(own, B_DEV))(jax.random.split(splits[6], SPANS)).reshape((SPANS, B_DEV)).astype(jnp.int32),
    }


norm_eps = 1e-06

def backward_head(unit_rows, radius_rows, step_rows, projection):
    radial_dot = lax.optimization_barrier(jnp.sum(unit_rows * step_rows, axis=1, keepdims=True))
    delta_rows = ((step_rows - unit_rows * radial_dot) / radius_rows).astype(jnp.bfloat16)
    return jnp.dot(delta_rows, projection.T, preferred_element_type=jnp.float32).astype(jnp.bfloat16)

def reference(picture_encoder_outputs, caption_encoder_outputs, picture_mapping_matrix, caption_mapping_matrix, scale_exponent_param, score_shift_param, partner_caption_row):
    img_raw = jnp.dot(picture_encoder_outputs, picture_mapping_matrix, preferred_element_type=jnp.float32)
    txt_raw = jnp.dot(caption_encoder_outputs, caption_mapping_matrix, preferred_element_type=jnp.float32)
    img_radius = jnp.sqrt(lax.optimization_barrier(jnp.sum(img_raw * img_raw, axis=1, keepdims=True)) + norm_eps)
    txt_radius = jnp.sqrt(lax.optimization_barrier(jnp.sum(txt_raw * txt_raw, axis=1, keepdims=True)) + norm_eps)
    img_unit = img_raw / img_radius
    txt_unit = txt_raw / txt_radius
    img_blocks = img_unit.astype(jnp.bfloat16).astype(jnp.float32).reshape(SPANS, B_DEV, E)
    txt_blocks = txt_unit.astype(jnp.bfloat16).astype(jnp.float32).reshape(SPANS, B_DEV, E)
    score_scale_factor = jnp.exp(scale_exponent_param[0])
    score_shift_scalar = score_shift_param[0]
    positive = partner_caption_row[:, :, None] == jnp.arange(B_DEV, dtype=jnp.int32)[None, None, :]
    img_grad_sum = jnp.zeros((SPANS, B_DEV, E), jnp.float32)
    txt_grad_sum = jnp.zeros((SPANS, B_DEV, E), jnp.float32)
    row_total = jnp.zeros((SPANS, B_DEV), jnp.float32)
    for offset in range(STEPS):
        partner = jnp.roll(txt_blocks, -offset, axis=0)
        angular_agreement = jnp.einsum('cie,cje->cij', img_blocks, partner)
        matched_scores = score_scale_factor * angular_agreement + score_shift_scalar
        if offset == 0:
            match_polarity = jnp.where(positive, 1.0, -1.0).astype(jnp.float32)
        else:
            match_polarity = -jnp.ones_like(matched_scores)
        row_total = row_total + lax.optimization_barrier(jnp.sum(jax.nn.softplus(-match_polarity * matched_scores), axis=2))
        squash_derivative = (-score_scale_factor * match_polarity * jax.nn.sigmoid(-match_polarity * matched_scores)).astype(jnp.bfloat16)
        squash_derivative = lax.optimization_barrier(squash_derivative).astype(jnp.float32)
        img_grad_sum = img_grad_sum + jnp.einsum('cij,cje->cie', squash_derivative, partner)
        txt_grad_sum = txt_grad_sum + jnp.roll(jnp.einsum('cij,cie->cje', squash_derivative, img_blocks), offset, axis=0)
    row_loss = (row_total / (STEPS * B_DEV)).reshape(TOKENS)
    img_grad = backward_head(img_unit, img_radius, img_grad_sum.reshape(TOKENS, E), picture_mapping_matrix)
    txt_grad = backward_head(txt_unit, txt_radius, txt_grad_sum.reshape(TOKENS, E), caption_mapping_matrix)
    return (img_grad, txt_grad, row_loss)
```

```python
import functools

import jax
import jax.numpy as jnp
from jax import lax
from jax.experimental import pallas as pl
from jax.experimental.pallas import tpu as pltpu
from jax.sharding import PartitionSpec as P

MESH = pl.DeviceIdType.MESH
STEPS = 8
VISITS = STEPS // 2
PARTS = 3
WIDE = 512

norm_eps = 1e-06
F32 = jnp.float32
BF16 = jnp.bfloat16

NN = (((1,), (0,)), ((), ()))
NT = (((1,), (1,)), ((), ()))


def mm(a, b, dims=NN):
    return lax.dot_general(a, b, dims, preferred_element_type=F32)


def kernel(
    n,
    xi_hbm, xt_hbm, wi_hbm, wt_hbm, scale_ref, shift_ref, partner_ref,
    gi_ref, gt_ref, loss_ref,
    x, w, psend, pown, precv, ysend, yrecv, unit, radius,
    a, b, slope, slope_t, da, rsend, rrecv,
    dbsend, dbown, dbrecv, y1send, y1recv, y0send, y0recv, xsend, xrecv,
    delta, lsend, lrecv, lstage, lpeer,
    load_sem, ss, rs,
):
    c = lax.axis_index("dp")
    m = lax.axis_index("mp")
    lo, k = m // 2, m % 2
    mq = (m + 2) % 4
    q = a.shape[0] // VISITS
    rows = 4 * q
    cols = w.shape[2]
    part = q // PARTS

    core = (c, m + 1 - 2 * k)
    near = (c, mq)
    prev = ((c + n - 1) % n, mq)
    after = ((c + 1) % n, mq)
    up = [((c + 2 * s) % n, m) for s in range(1, VISITS)]
    down = [((c + n - 2 * s) % n, m) for s in range(1, VISITS)]

    loads = []
    for i, (src, dst) in enumerate(
        [(xi_hbm, x.at[0]), (wi_hbm, w.at[0]), (xt_hbm, x.at[1]), (wt_hbm, w.at[1])]
    ):
        load = pltpu.make_async_copy(src, dst, load_sem.at[i])
        load.start()
        loads.append(load)

    barrier = pltpu.get_barrier_semaphore()
    peers = [core, near, prev, after] + up + [down[0]]
    for peer in peers:
        pl.semaphore_signal(barrier, inc=1, device_id=peer, device_id_type=MESH)

    count = [0]
    sent = []

    def message(src, dst, target):
        i = count[0]
        count[0] += 1
        return pltpu.make_async_remote_copy(
            src_ref=src, dst_ref=dst, send_sem=ss.at[i], recv_sem=rs.at[i],
            device_id=target, device_id_type=MESH,
        )

    def send(copy):
        copy.start()
        sent.append(copy)
        return copy

    def at(start, size):
        return pl.ds(pl.multiple_of(start, 16), size)

    def quarter(j):
        return at(j * q, q)

    def piece(j):
        return pl.ds(j * part, part)

    def spans():
        return [slice(i, i + WIDE) for i in range(0, cols, WIDE)]

    def project(t, which, out, to):
        left = jnp.concatenate([x[t, quarter(which), :], x[t, quarter(which + 2), :]], axis=0)
        for span in spans():
            out[t, :, span] = mm(left, w[t, :, span]).astype(to)

    first = []
    for t in range(2):
        loads[2 * t].wait()
        loads[2 * t + 1].wait()
        project(t, 1 - k, psend, BF16)
        if t == 0:
            pl.semaphore_wait(barrier, len(peers))
        first.append(send(message(psend.at[t], precv.at[t], core)))
        project(t, k, pown, F32)

    second = []
    for t in range(2):
        first[t].wait_recv()
        ysend[t] = (
            pown[t, quarter(1 - lo), :] + precv[t, quarter(1 - lo), :].astype(F32)
        ).astype(BF16)
        second.append(send(message(ysend.at[t], yrecv.at[t], near)))

    def normalise(t):
        raw = (
            pown[t, quarter(lo), :]
            + precv[t, quarter(lo), :].astype(F32)
            + yrecv[t].astype(F32)
        )
        size = jnp.sqrt(jnp.sum(raw * raw, axis=1, keepdims=True) + norm_eps)
        value = raw / size
        unit[t] = value
        radius[t] = jnp.broadcast_to(size, radius.shape[1:])
        return value.astype(BF16)

    second[0].wait_recv()
    a[0:q] = normalise(0)

    def visit(s, j):
        return message(
            a.at[pl.ds(s * q + j * part, part)], a.at[pl.ds((s + 1) * q + j * part, part)], up[0]
        )

    hops = [[visit(s, j) for j in range(PARTS)] for s in range(VISITS - 1)]
    for hop in hops[0]:
        send(hop)

    second[1].wait_recv()
    b[quarter(m)] = normalise(1)

    def text(block, j, into, target, size=q, skip=0):
        return message(
            b.at[at(block * rows + j * q + skip, size)],
            b.at[at(into * rows + j * q + skip, size)],
            target,
        )

    across = [send(text(0, m, 1, prev, part, j * part)) for j in range(PARTS)]
    beside = [send(text(0, m, 0, near, part, j * part)) for j in range(PARTS)]
    in_chip = [send(text(0, m, 0, core))]

    for j in range(PARTS):
        hops[0][j].wait_recv()
        send(hops[1][j])

    relay = []
    for j in range(PARTS):
        across[j].wait_recv()
        relay.append(send(text(1, mq, 1, near, part, j * part)))
    in_chip.append(send(text(1, mq, 1, core)))
    for j in range(PARTS):
        beside[j].wait_recv()
    in_chip.append(send(text(0, mq, 0, core)))
    for j in range(PARTS):
        hops[1][j].wait_recv()
        send(hops[2][j])
    for j in range(PARTS):
        relay[j].wait_recv()
    in_chip.append(send(text(1, m, 1, core)))
    for copy in in_chip:
        copy.wait_recv()
    for j in range(PARTS):
        hops[2][j].wait_recv()

    temperature = jnp.exp(jnp.full((q, 2 * rows), scale_ref[0], F32))
    shift = shift_ref[0]
    named = (
        lax.broadcasted_iota(jnp.int32, (2 * rows, rows), 0) == partner_ref[...]
    ).astype(BF16)
    own = (
        lax.broadcasted_iota(jnp.int32, (q, rows), 1)
        == lax.broadcasted_iota(jnp.int32, (q, rows), 0) + m * q
    )
    positive = mm(own.astype(BF16), named, NT) > 0.5
    scores = mm(a[...], b[...], NT)
    losses = []
    for s in range(VISITS):
        logits = temperature * scores[s * q:(s + 1) * q] + shift
        z = jnp.where(positive, -logits, logits) if s == 0 else logits
        u = jnp.exp(-jnp.abs(z))
        soft = jnp.maximum(z, 0.0) + jnp.log1p(u)
        sig = jnp.where(z >= 0.0, 1.0, u) / (1.0 + u)
        grade = temperature * sig
        if s == 0:
            grade = jnp.where(positive, -grade, grade)
        slope[s * q:(s + 1) * q] = grade.astype(BF16)
        slope_t[:, s * q:(s + 1) * q] = grade.T.astype(BF16)
        losses.append(jnp.sum(soft, axis=1, keepdims=True))

    last = VISITS - 1
    far = slope[last * q:]
    for span in spans():
        rsend[last - 1, :, span] = mm(far, b[:, span]).astype(BF16)

    def homeward(s, j):
        return message(rsend.at[s - 1, piece(j)], rrecv.at[s - 1, piece(j)], down[0])

    ways = {s: [homeward(s, j) for j in range(PARTS)] for s in range(1, VISITS)}
    for way in ways[last]:
        send(way)

    def text_side(which):
        return jnp.concatenate([slope_t[at(i * 2 * q + which * q, q)] for i in range(4)], axis=0)

    left = text_side(1 - k)
    for span in spans():
        dbsend[:, span] = mm(left, a[:, span]).astype(BF16)
    swap = send(message(dbsend, dbrecv, core))
    left = text_side(k)
    for span in spans():
        dbown[:, span] = mm(left, a[:, span])
    for span in spans():
        da[:, span] = mm(slope[:last * q], b[:, span])

    spread = (
        lax.broadcasted_iota(jnp.int32, (q, lsend.shape[2]), 1)
        == lax.broadcasted_iota(jnp.int32, (q, lsend.shape[2]), 0) + m * q
    )

    def as_lanes(column):
        line = jnp.sum(jnp.where(spread, column, 0.0), axis=0, keepdims=True)
        return jnp.broadcast_to(line, lsend.shape[1:])

    home = []
    for s in range(1, VISITS):
        lsend[s - 1] = as_lanes(losses[s])
        home.append(send(message(lsend.at[s - 1], lrecv.at[s - 1], down[s - 1])))

    swap.wait_recv()

    def chip_sum(block, half):
        where = at((2 * block + half) * q, q)
        return dbown[where] + dbrecv[where].astype(F32)

    y1send[...] = chip_sum(1, lo).astype(BF16)
    beside1 = [
        send(message(y1send.at[piece(j)], y1recv.at[piece(j)], near)) for j in range(PARTS)
    ]
    y0send[...] = chip_sum(0, 1 - lo).astype(BF16)
    beside0 = send(message(y0send, y0recv, near))

    def add_way(s, j):
        ways[s + 1][j].wait_recv()
        at_home = pl.ds(s * q + j * part, part)
        total = da[at_home] + rrecv[s, piece(j)].astype(F32)
        return total

    for j in range(PARTS):
        rsend[1, piece(j)] = add_way(2, j).astype(BF16)
        send(ways[2][j])

    over = []
    for j in range(PARTS):
        beside1[j].wait_recv()
        where = at((2 + 1 - lo) * q + j * part, part)
        xsend[piece(j)] = (
            dbown[where] + dbrecv[where].astype(F32) + y1recv[piece(j)].astype(F32)
        ).astype(BF16)
        over.append(send(message(xsend.at[piece(j)], xrecv.at[piece(j)], after)))

    total = as_lanes(losses[0])
    for s in range(1, VISITS):
        home[s - 1].wait_recv()
        total = total + lrecv[s - 1]
    lstage[0] = total
    pair = send(message(lstage.at[0], lpeer.at[0], core))

    for j in range(PARTS):
        rsend[0, piece(j)] = add_way(1, j).astype(BF16)
        send(ways[1][j])

    pair.wait_recv()
    lstage[1] = lstage[0] + lpeer[0]
    pair = send(message(lstage.at[1], lpeer.at[1], near))

    def tangent(t, step, where):
        vec = unit[t, where]
        radial = jnp.sum(vec * step, axis=1, keepdims=True)
        return ((step - vec * radial) / radius[t, where, 0:1]).astype(BF16)

    def gather(t, j, target, size=q, skip=0):
        where = at(j * q + skip, size)
        return message(delta.at[t, where], delta.at[t, where], target)

    beside0.wait_recv()
    for copy in over:
        copy.wait_recv()
    step = chip_sum(0, lo) + y0recv[...].astype(F32) + xrecv[...].astype(F32)
    delta[1, quarter(m)] = tangent(1, step, slice(0, q))
    text_near = send(gather(1, m, near))
    text_core = [send(gather(1, m, core))]

    image_near = []
    for j in range(PARTS):
        step = add_way(0, j)
        delta[0, at(m * q + j * part, part)] = tangent(0, step, piece(j))
        image_near.append(send(gather(0, m, near, part, j * part)))
    image_core = [send(gather(0, m, core))]

    text_near.wait_recv()
    text_core.append(send(gather(1, mq, core)))
    pair.wait_recv()
    loss = (lstage[1] + lpeer[1]) * (1.0 / (STEPS * rows))
    loss_ref[...] = loss[0:1, 0:rows]
    for copy in text_core:
        copy.wait_recv()
    gt_ref[...] = mm(delta[1], w[1], NT).astype(BF16)

    for copy in image_near:
        copy.wait_recv()
    image_core.append(send(gather(0, mq, core)))
    for copy in image_core:
        copy.wait_recv()
    gi_ref[...] = mm(delta[0], w[0], NT).astype(BF16)

    for copy in sent:
        copy.wait_send()


def shards(n, xi, xt, wi, wt, scale, shift, partner):
    rows, share = xi.shape
    cols = wi.shape[1]
    q = rows // 4
    vm = pltpu.VMEM
    lanes = -(-rows // 128) * 128
    messages = 64
    gi, gt, loss = pl.pallas_call(
        functools.partial(kernel, n),
        out_shape=(
            jax.ShapeDtypeStruct((rows, share), BF16),
            jax.ShapeDtypeStruct((rows, share), BF16),
            jax.ShapeDtypeStruct((1, rows), F32),
        ),
        in_specs=[pl.BlockSpec(memory_space=pl.ANY)] * 4
        + [pl.BlockSpec(memory_space=pltpu.SMEM)] * 2
        + [pl.BlockSpec(memory_space=pltpu.VMEM)],
        out_specs=(pl.BlockSpec(memory_space=pltpu.VMEM),) * 3,
        scratch_shapes=[
            vm((2, rows, share), BF16),
            vm((2, share, cols), BF16),
            vm((2, 2 * q, cols), BF16),
            vm((2, 2 * q, cols), F32),
            vm((2, 2 * q, cols), BF16),
            vm((2, q, cols), BF16),
            vm((2, q, cols), BF16),
            vm((2, q, cols), F32),
            vm((2, q, 128), F32),
            vm((VISITS * q, cols), BF16),
            vm((2 * rows, cols), BF16),
            vm((VISITS * q, 2 * rows), BF16),
            vm((2 * rows, VISITS * q), BF16),
            vm(((VISITS - 1) * q, cols), F32),
            vm((VISITS - 1, q, cols), BF16),
            vm((VISITS - 1, q, cols), BF16),
            vm((4 * q, cols), BF16),
            vm((4 * q, cols), F32),
            vm((4 * q, cols), BF16),
            vm((q, cols), BF16),
            vm((q, cols), BF16),
            vm((q, cols), BF16),
            vm((q, cols), BF16),
            vm((q, cols), BF16),
            vm((q, cols), BF16),
            vm((2, rows, cols), BF16),
            vm((VISITS - 1, 8, lanes), F32),
            vm((VISITS - 1, 8, lanes), F32),
            vm((2, 8, lanes), F32),
            vm((2, 8, lanes), F32),
            pltpu.SemaphoreType.DMA((4,)),
            pltpu.SemaphoreType.DMA((messages,)),
            pltpu.SemaphoreType.DMA((messages,)),
        ],
        compiler_params=pltpu.CompilerParams(
            collective_id=0, has_side_effects=True, vmem_limit_bytes=48 * 2**20
        ),
    )(xi, xt, wi, wt, scale, shift, partner)
    return gi, gt, loss.reshape(rows)


def solution(mesh):
    placed = (P("dp", "mp"), P("dp", "mp"), P("mp", None), P("mp", None), P(), P(), P("dp", None))
    return jax.shard_map(
        functools.partial(shards, mesh.shape["dp"]),
        mesh=mesh,
        in_specs=placed,
        out_specs=(P("dp", "mp"), P("dp", "mp"), P("dp")),
        check_vma=False,
    )
```

```python
import functools

import jax
import jax.numpy as jnp
from jax import lax
from jax.experimental import pallas as pl
from jax.experimental.pallas import tpu as pltpu
from jax.sharding import PartitionSpec as P

MESH = pl.DeviceIdType.MESH
STEPS = 8
VISITS = STEPS // 2
PARTS = 3
WIDE = 512

norm_eps = 1e-06
F32 = jnp.float32
BF16 = jnp.bfloat16

NN = (((1,), (0,)), ((), ()))
NT = (((1,), (1,)), ((), ()))


def mm(a, b, dims=NN):
    return lax.dot_general(a, b, dims, preferred_element_type=F32)


def spans(cols):
    return [slice(i, i + WIDE) for i in range(0, cols, WIDE)]


def kernel(
    n,
    xi_hbm, xt_hbm, wi_hbm, wt_hbm, scale_hbm, shift_hbm, partner_hbm,
    gi_hbm, gt_hbm, loss_hbm,
    gi_ref, gt_ref, loss_ref, x, w, partner_ref, scale_ref, shift_ref, psend, pown, precv, ysend, yrecv, unit, radius,
    a, b, slope, slope_t, da, rsend, rrecv,
    dbsend, dbown, dbrecv, y1send, y1recv, y0send, y0recv, xsend, xrecv,
    delta, lsend, lrecv, lstage, lpeer,
    load_sem, out_sem, ss, rs,
):
    c = lax.axis_index("dp")
    m = lax.axis_index("mp")
    lo, k = m // 2, m % 2
    mq = (m + 2) % 4
    q = a.shape[0] // VISITS
    rows = 4 * q
    cols = w.shape[2]
    part = q // PARTS

    core = (c, m + 1 - 2 * k)
    near = (c, mq)
    prev = ((c + n - 1) % n, mq)
    after = ((c + 1) % n, mq)
    up = ((c + 2) % n, m)
    down = [((c + n - 2 * s) % n, m) for s in range(1, VISITS)]

    loads = {}
    for i, (name, src, dst) in enumerate(
        [("x0", xi_hbm, x.at[0])]
        + [(f"w0{j}", wi_hbm.at[:, span], w.at[0, :, span]) for j, span in enumerate(spans(cols))]
        + [("x1", xt_hbm, x.at[1])]
        + [(f"w1{j}", wt_hbm.at[:, span], w.at[1, :, span]) for j, span in enumerate(spans(cols))]
        + [("p", partner_hbm, partner_ref), ("t", scale_hbm, scale_ref), ("b", shift_hbm, shift_ref)]
    ):
        loads[name] = pltpu.make_async_copy(src, dst, load_sem.at[i])
        loads[name].start()

    barrier = pltpu.get_barrier_semaphore()
    peers = [core, near, prev, after, up, down[0]]
    for peer in peers:
        pl.semaphore_signal(barrier, inc=1, device_id=peer, device_id_type=MESH)

    count = [0]
    sent = []

    def message(src, dst, target):
        i = count[0]
        count[0] += 1
        return pltpu.make_async_remote_copy(
            src_ref=src, dst_ref=dst, send_sem=ss.at[i], recv_sem=rs.at[i],
            device_id=target, device_id_type=MESH,
        )

    def send(copy):
        copy.start()
        sent.append(copy)
        return copy

    def drain():
        for copy in sent:
            copy.wait_send()
        sent.clear()

    def at(start, size):
        return pl.ds(pl.multiple_of(start, 16), size)

    def piece(j, base=0):
        return pl.ds(base + j * part, part)

    pieces = range(PARTS)

    def project(t, chip, which, out, to, ready=False):
        left = x[t, at((2 * chip + which) * q, q), :]
        for j, span in enumerate(spans(cols)):
            if not ready:
                loads[f"w{t}{j}"].wait()
            out[:, span] = mm(left, w[t, :, span]).astype(to)

    first = [[None, None], [None, None]]
    for t in range(2):
        loads[f"x{t}"].wait()
        project(t, 1 - lo, 1 - k, psend.at[t, 0], BF16)
        if t == 0:
            pl.semaphore_wait(barrier, len(peers))
        first[t][0] = send(message(psend.at[t, 0], precv.at[t, 0], core))
    for t in range(2):
        project(t, 1 - lo, k, pown.at[t, 0], F32, True)
    project(0, lo, 1 - k, psend.at[0, 1], BF16, True)
    first[0][1] = send(message(psend.at[0, 1], precv.at[0, 1], core))

    second = [[], []]

    def over_y(t):
        first[t][0].wait_recv()
        for j in pieces:
            here = piece(j)
            ysend[t, here] = (pown[t, 0, here] + precv[t, 0, here].astype(F32)).astype(BF16)
            second[t].append(send(message(ysend.at[t, here], yrecv.at[t, here], near)))

    over_y(0)
    over_y(1)
    project(1, lo, 1 - k, psend.at[1, 1], BF16, True)
    first[1][1] = send(message(psend.at[1, 1], precv.at[1, 1], core))
    for t in range(2):
        project(t, lo, k, pown.at[t, 1], F32, True)

    def normalise(t, j):
        here = piece(j)
        second[t][j].wait_recv()
        raw = pown[t, 1, here] + precv[t, 1, here].astype(F32) + yrecv[t, here].astype(F32)
        size = jnp.sqrt(jnp.sum(raw * raw, axis=1, keepdims=True) + norm_eps)
        value = raw / size
        unit[t, here] = value
        radius[t, here] = jnp.broadcast_to(size, (part, radius.shape[2]))
        return value.astype(BF16)

    def visit(s, j):
        return message(a.at[piece(j, s * q)], a.at[piece(j, (s + 1) * q)], up)

    def text(into, j, target, size=q, skip=0, block=None):
        block = into if block is None else block
        return message(
            b.at[at(block * rows + j * q + skip, size)],
            b.at[at(into * rows + j * q + skip, size)],
            target,
        )

    hops = [[visit(s, j) for j in pieces] for s in range(VISITS - 1)]
    first[0][1].wait_recv()
    for j in pieces:
        a[piece(j)] = normalise(0, j)
        send(hops[0][j])

    first[1][1].wait_recv()
    across, beside, relay, in_chip = [], [], [], []
    for j in pieces:
        b[at(m * q + j * part, part)] = normalise(1, j)
        across.append(send(text(1, m, prev, part, j * part, block=0)))
        beside.append(send(text(0, m, near, part, j * part)))
        hops[0][j].wait_recv()
        send(hops[1][j])
    in_chip.append(send(text(0, m, core)))
    for j in pieces:
        across[j].wait_recv()
        relay.append(send(text(1, mq, near, part, j * part)))
        hops[1][j].wait_recv()
        send(hops[2][j])
    in_chip.append(send(text(1, mq, core)))
    for j in pieces:
        beside[j].wait_recv()
    in_chip.append(send(text(0, mq, core)))

    for name in "ptb":
        loads[name].wait()
    temperature = jnp.exp(jnp.full((q, 2 * rows), scale_ref[0], F32))
    shift = shift_ref[0]
    named = (
        lax.broadcasted_iota(jnp.int32, (2 * rows, rows), 0) == partner_ref[...]
    ).astype(BF16)
    own = (
        lax.broadcasted_iota(jnp.int32, (q, rows), 1)
        == lax.broadcasted_iota(jnp.int32, (q, rows), 0) + m * q
    )
    positive = mm(own.astype(BF16), named, NT) > 0.5
    drain()

    for j in pieces:
        relay[j].wait_recv()
        in_chip.append(send(text(1, m, core, part, j * part)))
    for j in pieces:
        hops[2][j].wait_recv()
    for copy in in_chip:
        copy.wait_recv()

    losses = {}
    last = VISITS - 1

    def score(s, scores):
        logits = temperature * scores + shift
        z = jnp.where(positive, -logits, logits) if s == 0 else logits
        u = jnp.exp(-jnp.abs(z))
        soft = jnp.maximum(z, 0.0) + jnp.log1p(u)
        sig = jnp.where(z >= 0.0, 1.0, u) / (1.0 + u)
        grade = temperature * sig
        if s == 0:
            grade = jnp.where(positive, -grade, grade)
        slope[s * q:(s + 1) * q] = grade.astype(BF16)
        slope_t[:, s * q:(s + 1) * q] = grade.T.astype(BF16)
        losses[s] = jnp.sum(soft, axis=1, keepdims=True)

    scores = mm(a[...], b[...], NT)
    score(last, scores[last * q:])

    far = slope[last * q:]
    for span in spans(cols):
        rsend[last - 1, :, span] = mm(far, b[:, span]).astype(BF16)

    def homeward(s, j):
        return message(rsend.at[s - 1, piece(j)], rrecv.at[s - 1, piece(j)], down[0])

    ways = {s: [homeward(s, j) for j in pieces] for s in range(1, VISITS)}
    for way in ways[last]:
        send(way)
    for s in range(last):
        score(s, scores[s * q:(s + 1) * q])

    def text_side(block, which):
        return jnp.concatenate(
            [slope_t[at((2 * block + half) * 2 * q + which * q, q)] for half in range(2)], axis=0
        )

    swap = {}
    for block in (1, 0):
        left = text_side(block, 1 - k)
        for span in spans(cols):
            dbsend[block, :, span] = mm(left, a[:, span]).astype(BF16)
        swap[block] = send(message(dbsend.at[block], dbrecv.at[block], core))
    for block in (1, 0):
        left = text_side(block, k)
        for span in spans(cols):
            dbown[block, :, span] = mm(left, a[:, span])

    def chip_sum(block, half, j):
        where = at(half * q + j * part, part)
        return dbown[block, where] + dbrecv[block, where].astype(F32)

    beside1, beside0, over = [], [], []
    swap[1].wait_recv()
    for j in pieces:
        y1send[piece(j)] = chip_sum(1, lo, j).astype(BF16)
        beside1.append(send(message(y1send.at[piece(j)], y1recv.at[piece(j)], near)))
    for span in spans(cols):
        da[:, span] = mm(slope[:last * q], b[:, span])
    swap[0].wait_recv()
    for j in pieces:
        y0send[piece(j)] = chip_sum(0, 1 - lo, j).astype(BF16)
        beside0.append(send(message(y0send.at[piece(j)], y0recv.at[piece(j)], near)))

    def add_way(s, j):
        ways[s + 1][j].wait_recv()
        return da[piece(j, s * q)] + rrecv[s, piece(j)].astype(F32)

    def onward(s, j):
        rsend[s - 1, piece(j)] = add_way(s, j).astype(BF16)
        send(ways[s][j])

    def cross(j):
        beside1[j].wait_recv()
        xsend[piece(j)] = (chip_sum(1, 1 - lo, j) + y1recv[piece(j)].astype(F32)).astype(BF16)
        over.append(send(message(xsend.at[piece(j)], xrecv.at[piece(j)], after)))

    spread = (
        lax.broadcasted_iota(jnp.int32, (q, lsend.shape[2]), 1)
        == lax.broadcasted_iota(jnp.int32, (q, lsend.shape[2]), 0) + m * q
    )

    def as_lanes(column):
        line = jnp.sum(jnp.where(spread, column, 0.0), axis=0, keepdims=True)
        return jnp.broadcast_to(line, lsend.shape[1:])

    for j in pieces:
        onward(2, j)
    home = []
    for s in range(1, VISITS):
        lsend[s - 1] = as_lanes(losses[s])
        home.append(send(message(lsend.at[s - 1], lrecv.at[s - 1], down[s - 1])))
    for j in pieces:
        cross(j)
        onward(1, j)

    total = as_lanes(losses[0])
    for s in range(1, VISITS):
        home[s - 1].wait_recv()
        total = total + lrecv[s - 1]
    lstage[0] = total
    pair = send(message(lstage.at[0], lpeer.at[0], core))

    def tangent(t, step, j):
        here = piece(j)
        vec = unit[t, here]
        radial = jnp.sum(vec * step, axis=1, keepdims=True)
        return ((step - vec * radial) / radius[t, here, 0:1]).astype(BF16)

    def gather(t, j, target, size=q, skip=0):
        where = at(j * q + skip, size)
        return message(delta.at[t, where], delta.at[t, where], target)

    beyond = [[], []]
    inside = [[], []]

    def text_step(j):
        beside0[j].wait_recv()
        over[j].wait_recv()
        step = chip_sum(0, lo, j) + y0recv[piece(j)].astype(F32) + xrecv[piece(j)].astype(F32)
        delta[1, at(m * q + j * part, part)] = tangent(1, step, j)
        beyond[1].append(send(gather(1, m, near, part, j * part)))

    def image_step(j):
        delta[0, at(m * q + j * part, part)] = tangent(0, add_way(0, j), j)
        beyond[0].append(send(gather(0, m, near, part, j * part)))

    for j in pieces:
        text_step(j)
        image_step(j)
    for t in (1, 0):
        inside[t].append(send(gather(t, m, core)))

    pair.wait_recv()
    lstage[1] = lstage[0] + lpeer[0]
    pair = send(message(lstage.at[1], lpeer.at[1], near))
    drain()

    half = 2 * q

    def result(t, out, chip):
        where = at(chip * half, half)
        out[where] = mm(delta[t, where], w[t], NT).astype(BF16)

    for t in (1, 0):
        inside[t][0].wait_recv()
    result(1, gt_ref, lo)
    result(0, gi_ref, lo)
    for j in pieces:
        for t in (1, 0):
            beyond[t][j].wait_recv()
            inside[t].append(send(gather(t, mq, core, part, j * part)))
    pair.wait_recv()
    loss = (lstage[1] + lpeer[1]) * (1.0 / (STEPS * rows))
    loss_ref[...] = loss[0, 0:rows]
    stores = []

    def put(src, dst):
        copy = pltpu.make_async_copy(src, dst, out_sem.at[len(stores)])
        copy.start()
        stores.append(copy)

    put(loss_ref, loss_hbm)
    for t, out, out_hbm in ((1, gt_ref, gt_hbm), (0, gi_ref, gi_hbm)):
        for copy in inside[t][1:]:
            copy.wait_recv()
        result(t, out, 1 - lo)
        put(out, out_hbm)
    drain()
    for copy in stores:
        copy.wait()


def store(gi, gt, loss, gi_out, gt_out, loss_out, gi_held, gt_held, loss_held, sem):
    held = (gi_held, gt_held, loss_held)
    ins = [pltpu.make_async_copy(s, d, sem.at[i]) for i, (s, d) in enumerate(zip((gi, gt, loss), held))]
    outs = [
        pltpu.make_async_copy(s, d, sem.at[3 + i])
        for i, (s, d) in enumerate(zip(held, (gi_out, gt_out, loss_out)))
    ]
    for copy in ins:
        copy.start()
    for into, out in zip(ins, outs):
        into.wait()
        out.start()
    for out in outs:
        out.wait()


def shards(n, xi, xt, wi, wt, scale, shift, partner):
    rows, share = xi.shape
    cols = wi.shape[1]
    q = rows // 4
    vm = pltpu.VMEM
    lanes = -(-rows // 128) * 128
    messages = 128
    gi, gt, loss = pl.pallas_call(
        functools.partial(kernel, n),
        out_shape=(
            jax.ShapeDtypeStruct((rows, share), BF16),
            jax.ShapeDtypeStruct((rows, share), BF16),
            jax.ShapeDtypeStruct((rows,), F32),
        ),
        in_specs=[pl.BlockSpec(memory_space=pl.ANY)] * 7,
        out_specs=(pl.BlockSpec(memory_space=pl.ANY),) * 3,
        scratch_shapes=[
            vm((rows, share), BF16),
            vm((rows, share), BF16),
            vm((rows,), F32),
            vm((2, rows, share), BF16),
            vm((2, share, cols), BF16),
            vm((1, rows), jnp.int32),
            pltpu.SMEM((1,), F32),
            pltpu.SMEM((1,), F32),
            vm((2, 2, q, cols), BF16),
            vm((2, 2, q, cols), F32),
            vm((2, 2, q, cols), BF16),
            vm((2, q, cols), BF16),
            vm((2, q, cols), BF16),
            vm((2, q, cols), F32),
            vm((2, q, 128), F32),
            vm((VISITS * q, cols), BF16),
            vm((2 * rows, cols), BF16),
            vm((VISITS * q, 2 * rows), BF16),
            vm((2 * rows, VISITS * q), BF16),
            vm(((VISITS - 1) * q, cols), F32),
            vm((VISITS - 1, q, cols), BF16),
            vm((VISITS - 1, q, cols), BF16),
            vm((2, 2 * q, cols), BF16),
            vm((2, 2 * q, cols), F32),
            vm((2, 2 * q, cols), BF16),
            vm((q, cols), BF16),
            vm((q, cols), BF16),
            vm((q, cols), BF16),
            vm((q, cols), BF16),
            vm((q, cols), BF16),
            vm((q, cols), BF16),
            vm((2, rows, cols), BF16),
            vm((VISITS - 1, 8, lanes), F32),
            vm((VISITS - 1, 8, lanes), F32),
            vm((2, 8, lanes), F32),
            vm((2, 8, lanes), F32),
            pltpu.SemaphoreType.DMA((16,)),
            pltpu.SemaphoreType.DMA((3,)),
            pltpu.SemaphoreType.DMA((messages,)),
            pltpu.SemaphoreType.DMA((messages,)),
        ],
        compiler_params=pltpu.CompilerParams(
            collective_id=0, has_side_effects=True, vmem_limit_bytes=62 * 2**20
        ),
    )(xi, xt, wi, wt, scale, shift, partner)
    return pl.pallas_call(
        store,
        out_shape=(
            jax.ShapeDtypeStruct((rows, share), BF16),
            jax.ShapeDtypeStruct((rows, share), BF16),
            jax.ShapeDtypeStruct((rows,), F32),
        ),
        in_specs=[pl.BlockSpec(memory_space=pl.ANY)] * 3,
        out_specs=(pl.BlockSpec(memory_space=pl.ANY),) * 3,
        scratch_shapes=[vm((rows, share), BF16), vm((rows, share), BF16), vm((rows,), F32), pltpu.SemaphoreType.DMA((6,))],
        compiler_params=pltpu.CompilerParams(vmem_limit_bytes=62 * 2**20),
    )(gi, gt, loss)


def solution(mesh):
    placed = (P("dp", "mp"), P("dp", "mp"), P("mp", None), P("mp", None), P(), P(), P("dp", None))
    return jax.shard_map(
        functools.partial(shards, mesh.shape["dp"]),
        mesh=mesh,
        in_specs=placed,
        out_specs=(P("dp", "mp"), P("dp", "mp"), P("dp")),
        check_vma=False,
    )
```

```python
import functools

import jax
import jax.numpy as jnp
from jax import lax
from jax.experimental import pallas as pl
from jax.experimental.pallas import tpu as pltpu
from jax.sharding import PartitionSpec as P

MESH = pl.DeviceIdType.MESH
STEPS = 8
VISITS = STEPS // 2
PARTS = 3
WIDE = 768

norm_eps = 1e-06
F32 = jnp.float32
BF16 = jnp.bfloat16

NN = (((1,), (0,)), ((), ()))
NT = (((1,), (1,)), ((), ()))


def mm(a, b, dims=NN):
    return lax.dot_general(a, b, dims, preferred_element_type=F32)


def spans(cols):
    return [slice(i, i + WIDE) for i in range(0, cols, WIDE)]


def kernel(
    n,
    xi_hbm, xt_hbm, wi_hbm, wt_hbm, scale_hbm, shift_hbm, partner_hbm,
    gi_hbm, gt_hbm, loss_hbm,
    gi_ref, gt_ref, loss_ref, x, w, partner_ref, scale_ref, shift_ref, psend, pown, precv, ysend, yrecv, unit, radius,
    a, b, slope, slope_t, da, rsend, rrecv,
    dbsend, dbown, dbrecv, y1send, y1recv, y0send, y0recv, xsend, xrecv,
    delta, lsend, lrecv, lstage, lpeer,
    load_sem, out_sem, ss, rs,
):
    c = lax.axis_index("dp")
    m = lax.axis_index("mp")
    lo, k = m // 2, m % 2
    mq = (m + 2) % 4
    q = a.shape[0] // VISITS
    rows = 4 * q
    cols = w.shape[2]
    part = q // PARTS

    core = (c, m + 1 - 2 * k)
    near = (c, mq)
    prev = ((c + n - 1) % n, mq)
    after = ((c + 1) % n, mq)
    prev_same = ((c + n - 1) % n, m)
    after_same = ((c + 1) % n, m)
    up = ((c + 2) % n, m)
    down = [((c + n - 2 * s) % n, m) for s in range(1, VISITS)]

    loads = {}
    for i, (name, src, dst) in enumerate(
        [("x0", xi_hbm, x.at[0])]
        + [(f"w0{j}", wi_hbm.at[:, span], w.at[0, :, span]) for j, span in enumerate(spans(cols))]
        + [("x1", xt_hbm, x.at[1])]
        + [(f"w1{j}", wt_hbm.at[:, span], w.at[1, :, span]) for j, span in enumerate(spans(cols))]
        + [("p", partner_hbm, partner_ref), ("t", scale_hbm, scale_ref), ("b", shift_hbm, shift_ref)]
    ):
        loads[name] = pltpu.make_async_copy(src, dst, load_sem.at[i])
        loads[name].start()

    barrier = pltpu.get_barrier_semaphore()
    peers = [core, near, prev, after, prev_same, after_same, up, down[0]]
    for peer in peers:
        pl.semaphore_signal(barrier, inc=1, device_id=peer, device_id_type=MESH)

    count = [0]
    sent = []

    def message(src, dst, target):
        i = count[0]
        count[0] += 1
        return pltpu.make_async_remote_copy(
            src_ref=src, dst_ref=dst, send_sem=ss.at[i], recv_sem=rs.at[i],
            device_id=target, device_id_type=MESH,
        )

    def send(copy):
        copy.start()
        sent.append(copy)
        return copy

    def drain():
        for copy in sent:
            copy.wait_send()
        sent.clear()

    def at(start, size):
        return pl.ds(pl.multiple_of(start, 16), size)

    def piece(j, base=0):
        return pl.ds(base + j * part, part)

    pieces = range(PARTS)

    def project(t, chip, which, out, to, ready=False):
        left = x[t, at((2 * chip + which) * q, q), :]
        for j, span in enumerate(spans(cols)):
            if not ready:
                loads[f"w{t}{j}"].wait()
            out[:, span] = mm(left, w[t, :, span]).astype(to)

    first = [[None, None], [None, None]]
    for t in range(2):
        loads[f"x{t}"].wait()
        project(t, 1 - lo, 1 - k, psend.at[t, 0], BF16)
        if t == 0:
            pl.semaphore_wait(barrier, len(peers))
        first[t][0] = send(message(psend.at[t, 0], precv.at[t, 0], core))
    for t in range(2):
        project(t, 1 - lo, k, pown.at[t, 0], F32, True)
    project(0, lo, 1 - k, psend.at[0, 1], BF16, True)
    first[0][1] = send(message(psend.at[0, 1], precv.at[0, 1], core))

    second = [[], []]

    def over_y(t):
        first[t][0].wait_recv()
        for j in pieces:
            here = piece(j)
            ysend[t, here] = (pown[t, 0, here] + precv[t, 0, here].astype(F32)).astype(BF16)
            second[t].append(send(message(ysend.at[t, here], yrecv.at[t, here], near)))

    over_y(0)
    over_y(1)
    project(1, lo, 1 - k, psend.at[1, 1], BF16, True)
    first[1][1] = send(message(psend.at[1, 1], precv.at[1, 1], core))
    for t in range(2):
        project(t, lo, k, pown.at[t, 1], F32, True)

    def normalise(t, j):
        here = piece(j)
        second[t][j].wait_recv()
        raw = pown[t, 1, here] + precv[t, 1, here].astype(F32) + yrecv[t, here].astype(F32)
        size = jnp.sqrt(jnp.sum(raw * raw, axis=1, keepdims=True) + norm_eps)
        value = raw / size
        unit[t, here] = value
        radius[t, here] = jnp.broadcast_to(size, (part, radius.shape[2]))
        return value.astype(BF16)

    def visit(s, j):
        return message(a.at[piece(j, s * q)], a.at[piece(j, (s + 1) * q)], up)

    def text(into, j, target, size=q, skip=0, block=None):
        block = into if block is None else block
        return message(
            b.at[at(block * rows + j * q + skip, size)],
            b.at[at(into * rows + j * q + skip, size)],
            target,
        )

    hops = [[visit(s, j) for j in pieces] for s in range(VISITS - 1)]
    first[0][1].wait_recv()
    for j in pieces:
        a[piece(j)] = normalise(0, j)
        send(hops[0][j])

    first[1][1].wait_recv()
    across, beside, relay, in_chip = [], [], [], []
    for j in pieces:
        b[at(m * q + j * part, part)] = normalise(1, j)
        across.append(send(text(1, m, prev, part, j * part, block=0)))
        beside.append(send(text(0, m, near, part, j * part)))
        hops[0][j].wait_recv()
        send(hops[1][j])
    in_chip.append(send(text(0, m, core)))
    for j in pieces:
        across[j].wait_recv()
        relay.append(send(text(1, mq, near, part, j * part)))
        hops[1][j].wait_recv()
        send(hops[2][j])
    in_chip.append(send(text(1, mq, core)))
    for j in pieces:
        beside[j].wait_recv()
    in_chip.append(send(text(0, mq, core)))

    for name in "ptb":
        loads[name].wait()
    temperature = jnp.exp(jnp.full((q, 2 * rows), scale_ref[0], F32))
    shift = shift_ref[0]
    named = (
        lax.broadcasted_iota(jnp.int32, (2 * rows, rows), 0) == partner_ref[...]
    ).astype(BF16)
    own = (
        lax.broadcasted_iota(jnp.int32, (q, rows), 1)
        == lax.broadcasted_iota(jnp.int32, (q, rows), 0) + m * q
    )
    positive = mm(own.astype(BF16), named, NT) > 0.5
    drain()

    for j in pieces:
        relay[j].wait_recv()
        in_chip.append(send(text(1, m, core, part, j * part)))
    for j in pieces:
        hops[2][j].wait_recv()
    for copy in in_chip:
        copy.wait_recv()

    losses = {}
    last = VISITS - 1

    def score(s, scores):
        logits = temperature * scores + shift
        z = jnp.where(positive, -logits, logits) if s == 0 else logits
        u = jnp.exp(-jnp.abs(z))
        soft = jnp.maximum(z, 0.0) + jnp.log1p(u)
        sig = jnp.where(z >= 0.0, 1.0, u) / (1.0 + u)
        grade = temperature * sig
        if s == 0:
            grade = jnp.where(positive, -grade, grade)
        slope[s * q:(s + 1) * q] = grade.astype(BF16)
        slope_t[:, s * q:(s + 1) * q] = grade.T.astype(BF16)
        losses[s] = jnp.sum(soft, axis=1, keepdims=True)

    scores = mm(a[...], b[...], NT)
    score(last, scores[last * q:])

    far = slope[last * q:]
    for span in spans(cols):
        rsend[last - 1, :, span] = mm(far, b[:, span]).astype(BF16)

    def homeward(s, j):
        return message(rsend.at[s - 1, piece(j)], rrecv.at[s - 1, piece(j)], down[0])

    ways = {s: [homeward(s, j) for j in pieces] for s in range(1, VISITS)}
    for way in ways[last]:
        send(way)
    for s in range(last):
        score(s, scores[s * q:(s + 1) * q])

    def text_side(block, which):
        return jnp.concatenate(
            [slope_t[at((2 * block + half) * 2 * q + which * q, q)] for half in range(2)], axis=0
        )

    swap = {}
    for block in (1, 0):
        left = text_side(block, 1 - k)
        for span in spans(cols):
            dbsend[block, :, span] = mm(left, a[:, span]).astype(BF16)
        swap[block] = send(message(dbsend.at[block], dbrecv.at[block], core))
    for block in (1, 0):
        left = text_side(block, k)
        for span in spans(cols):
            dbown[block, :, span] = mm(left, a[:, span])

    def chip_sum(block, half, j):
        where = at(half * q + j * part, part)
        return dbown[block, where] + dbrecv[block, where].astype(F32)

    skew, beside0, over = [], [], []
    swap[1].wait_recv()
    for j in pieces:
        here = piece(j)
        y1send[here] = chip_sum(1, lo, j).astype(BF16)
        skew.append(send(message(y1send.at[here], y1recv.at[here], after_same)))
        xsend[here] = chip_sum(1, 1 - lo, j).astype(BF16)
        over.append(send(message(xsend.at[here], xrecv.at[here], after)))
    swap[0].wait_recv()
    for j in pieces:
        here = piece(j)
        y0send[here] = chip_sum(0, 1 - lo, j).astype(BF16)
        beside0.append(send(message(y0send.at[here], y0recv.at[here], near)))
    for span in spans(cols):
        da[:, span] = mm(slope[:last * q], b[:, span])

    def add_way(s, j):
        ways[s + 1][j].wait_recv()
        return da[piece(j, s * q)] + rrecv[s, piece(j)].astype(F32)

    def onward(s, j):
        rsend[s - 1, piece(j)] = add_way(s, j).astype(BF16)
        send(ways[s][j])

    spread = (
        lax.broadcasted_iota(jnp.int32, (q, lsend.shape[2]), 1)
        == lax.broadcasted_iota(jnp.int32, (q, lsend.shape[2]), 0) + m * q
    )

    def as_lanes(column):
        line = jnp.sum(jnp.where(spread, column, 0.0), axis=0, keepdims=True)
        return jnp.broadcast_to(line, lsend.shape[1:])

    for j in pieces:
        onward(2, j)
    home = []
    for s in range(1, VISITS):
        lsend[s - 1] = as_lanes(losses[s])
        home.append(send(message(lsend.at[s - 1], lrecv.at[s - 1], down[s - 1])))
    def tangent(t, step, j):
        here = piece(j)
        vec = unit[t, here]
        radial = jnp.sum(vec * step, axis=1, keepdims=True)
        return ((step - vec * radial) / radius[t, here, 0:1]).astype(BF16)

    def gather(t, j, target, size=q, skip=0):
        where = at(j * q + skip, size)
        return message(delta.at[t, where], delta.at[t, where], target)

    beyond = [[], []]
    inside = [[], []]

    def text_step(j):
        here = piece(j)
        skew[j].wait_recv()
        over[j].wait_recv()
        beside0[j].wait_recv()
        step = chip_sum(0, lo, j) + y0recv[here].astype(F32)
        step = step + (xrecv[here].astype(F32) + y1recv[here].astype(F32))
        delta[1, at(m * q + j * part, part)] = tangent(1, step, j)
        beyond[1].append(send(gather(1, m, near, part, j * part)))

    def image_step(j):
        delta[0, at(m * q + j * part, part)] = tangent(0, add_way(0, j), j)
        beyond[0].append(send(gather(0, m, near, part, j * part)))

    for j in pieces:
        onward(1, j)
        text_step(j)
    inside[1].append(send(gather(1, m, core)))

    total = as_lanes(losses[0])
    for s in range(1, VISITS):
        home[s - 1].wait_recv()
        total = total + lrecv[s - 1]
    lstage[0] = total
    pair = send(message(lstage.at[0], lpeer.at[0], core))

    for j in pieces:
        image_step(j)
    inside[0].append(send(gather(0, m, core)))

    pair.wait_recv()
    lstage[1] = lstage[0] + lpeer[0]
    pair = send(message(lstage.at[1], lpeer.at[1], near))
    drain()

    half = 2 * q

    def result(t, out, chip):
        where = at(chip * half, half)
        out[where] = mm(delta[t, where], w[t], NT).astype(BF16)

    for t in (1, 0):
        inside[t][0].wait_recv()
    for j in pieces:
        beyond[1][j].wait_recv()
        inside[1].append(send(gather(1, mq, core, part, j * part)))
    result(1, gt_ref, lo)
    result(0, gi_ref, lo)
    for j in pieces:
        beyond[0][j].wait_recv()
        inside[0].append(send(gather(0, mq, core, part, j * part)))
    pair.wait_recv()
    loss = (lstage[1] + lpeer[1]) * (1.0 / (STEPS * rows))
    loss_ref[...] = loss[0, 0:rows]
    stores = []

    def put(src, dst):
        copy = pltpu.make_async_copy(src, dst, out_sem.at[len(stores)])
        copy.start()
        stores.append(copy)

    put(loss_ref, loss_hbm)
    for t, out, out_hbm in ((1, gt_ref, gt_hbm), (0, gi_ref, gi_hbm)):
        for copy in inside[t][1:]:
            copy.wait_recv()
        result(t, out, 1 - lo)
        put(out, out_hbm)
    drain()
    for copy in stores:
        copy.wait()


def store(gi, gt, loss, gi_out, gt_out, loss_out, gi_held, gt_held, loss_held, sem):
    held = (gi_held, gt_held, loss_held)
    ins = [pltpu.make_async_copy(s, d, sem.at[i]) for i, (s, d) in enumerate(zip((gi, gt, loss), held))]
    outs = [
        pltpu.make_async_copy(s, d, sem.at[3 + i])
        for i, (s, d) in enumerate(zip(held, (gi_out, gt_out, loss_out)))
    ]
    for copy in ins:
        copy.start()
    for into, out in zip(ins, outs):
        into.wait()
        out.start()
    for out in outs:
        out.wait()


def shards(n, xi, xt, wi, wt, scale, shift, partner):
    rows, share = xi.shape
    cols = wi.shape[1]
    q = rows // 4
    vm = pltpu.VMEM
    lanes = -(-rows // 128) * 128
    messages = 128
    gi, gt, loss = pl.pallas_call(
        functools.partial(kernel, n),
        out_shape=(
            jax.ShapeDtypeStruct((rows, share), BF16),
            jax.ShapeDtypeStruct((rows, share), BF16),
            jax.ShapeDtypeStruct((rows,), F32),
        ),
        in_specs=[pl.BlockSpec(memory_space=pl.ANY)] * 7,
        out_specs=(pl.BlockSpec(memory_space=pl.ANY),) * 3,
        scratch_shapes=[
            vm((rows, share), BF16),
            vm((rows, share), BF16),
            vm((rows,), F32),
            vm((2, rows, share), BF16),
            vm((2, share, cols), BF16),
            vm((1, rows), jnp.int32),
            pltpu.SMEM((1,), F32),
            pltpu.SMEM((1,), F32),
            vm((2, 2, q, cols), BF16),
            vm((2, 2, q, cols), F32),
            vm((2, 2, q, cols), BF16),
            vm((2, q, cols), BF16),
            vm((2, q, cols), BF16),
            vm((2, q, cols), F32),
            vm((2, q, 128), F32),
            vm((VISITS * q, cols), BF16),
            vm((2 * rows, cols), BF16),
            vm((VISITS * q, 2 * rows), BF16),
            vm((2 * rows, VISITS * q), BF16),
            vm(((VISITS - 1) * q, cols), F32),
            vm((VISITS - 1, q, cols), BF16),
            vm((VISITS - 1, q, cols), BF16),
            vm((2, 2 * q, cols), BF16),
            vm((2, 2 * q, cols), F32),
            vm((2, 2 * q, cols), BF16),
            vm((q, cols), BF16),
            vm((q, cols), BF16),
            vm((q, cols), BF16),
            vm((q, cols), BF16),
            vm((q, cols), BF16),
            vm((q, cols), BF16),
            vm((2, rows, cols), BF16),
            vm((VISITS - 1, 8, lanes), F32),
            vm((VISITS - 1, 8, lanes), F32),
            vm((2, 8, lanes), F32),
            vm((2, 8, lanes), F32),
            pltpu.SemaphoreType.DMA((16,)),
            pltpu.SemaphoreType.DMA((3,)),
            pltpu.SemaphoreType.DMA((messages,)),
            pltpu.SemaphoreType.DMA((messages,)),
        ],
        compiler_params=pltpu.CompilerParams(
            collective_id=0, has_side_effects=True, vmem_limit_bytes=62 * 2**20
        ),
    )(xi, xt, wi, wt, scale, shift, partner)
    return pl.pallas_call(
        store,
        out_shape=(
            jax.ShapeDtypeStruct((rows, share), BF16),
            jax.ShapeDtypeStruct((rows, share), BF16),
            jax.ShapeDtypeStruct((rows,), F32),
        ),
        in_specs=[pl.BlockSpec(memory_space=pl.ANY)] * 3,
        out_specs=(pl.BlockSpec(memory_space=pl.ANY),) * 3,
        scratch_shapes=[vm((rows, share), BF16), vm((rows, share), BF16), vm((rows,), F32), pltpu.SemaphoreType.DMA((6,))],
        compiler_params=pltpu.CompilerParams(vmem_limit_bytes=62 * 2**20),
    )(gi, gt, loss)


def solution(mesh):
    placed = (P("dp", "mp"), P("dp", "mp"), P("mp", None), P("mp", None), P(), P(), P("dp", None))
    return jax.shard_map(
        functools.partial(shards, mesh.shape["dp"]),
        mesh=mesh,
        in_specs=placed,
        out_specs=(P("dp", "mp"), P("dp", "mp"), P("dp")),
        check_vma=False,
    )
```

```python
import functools

import jax
import jax.numpy as jnp
from jax import lax
from jax.experimental import pallas as pl
from jax.experimental.pallas import tpu as pltpu
from jax.sharding import PartitionSpec as P

MESH = pl.DeviceIdType.MESH
STEPS = 8
VISITS = STEPS // 2
MESSAGES = 73
LEAVING = 24
PARTS = 3
CUTS = 1

norm_eps = 1e-06
F32 = jnp.float32
BF16 = jnp.bfloat16

NN = (((1,), (0,)), ((), ()))
NT = (((1,), (1,)), ((), ()))


def mm(a, b, dims=NN):
    return lax.dot_general(a, b, dims, preferred_element_type=F32)


def kernel(
    n,
    xi_hbm, xt_hbm, wi_hbm, wt_hbm, scale_hbm, shift_hbm, partner_hbm,
    gi_hbm, gt_hbm, loss_hbm,
    gi_ref, gt_ref, loss_ref, x, w, partner_ref, scale_ref, shift_ref, psend, pown, precv, ysend, yrecv, unit, radius,
    a, b, slope, slope_t, da, rsend, rrecv,
    dbsend, dbown, dbrecv, y1send, y1recv, y0send, y0recv, xsend, xrecv,
    delta, lsend, lrecv, lstage, lpeer,
    load_sem, out_sem, ss, rs,
):
    c = lax.axis_index("dp")
    m = lax.axis_index("mp")
    lo, k = m // 2, m % 2
    mq = (m + 2) % 4
    q = a.shape[1] // VISITS
    rows = 4 * q
    wide = w.shape[3]
    part = q // PARTS

    core = (c, m + 1 - 2 * k)
    near = (c, mq)
    prev = ((c + n - 1) % n, mq)
    after = ((c + 1) % n, mq)
    prev_same = ((c + n - 1) % n, m)
    after_same = ((c + 1) % n, m)
    up = ((c + 2) % n, m)
    down = [((c + n - 2 * s) % n, m) for s in range(1, VISITS)]

    loads = {}
    for i, (name, src, dst) in enumerate(
        [("x0", xi_hbm, x.at[0])]
        + [(f"w0{h}", wi_hbm.at[:, pl.ds(h * wide, wide)], w.at[0, h]) for h in range(CUTS)]
        + [("x1", xt_hbm, x.at[1])]
        + [(f"w1{h}", wt_hbm.at[:, pl.ds(h * wide, wide)], w.at[1, h]) for h in range(CUTS)]
        + [("p", partner_hbm, partner_ref), ("t", scale_hbm, scale_ref), ("b", shift_hbm, shift_ref)]
    ):
        loads[name] = pltpu.make_async_copy(src, dst, load_sem.at[i])
        loads[name].start()

    barrier = pltpu.get_barrier_semaphore()
    peers = [core, near, prev, after, prev_same, after_same, up, down[0]]
    for peer in peers:
        pl.semaphore_signal(barrier, inc=1, device_id=peer, device_id_type=MESH)

    slots = {}
    leaving = {}

    def message(src, dst, target):
        i = len(slots)
        copy = pltpu.make_async_remote_copy(
            src_ref=src, dst_ref=dst, send_sem=ss.at[i % LEAVING], recv_sem=rs.at[i],
            device_id=target, device_id_type=MESH,
        )
        slots[i] = copy
        return copy

    def send(copy):
        slot = next(i for i, other in slots.items() if other is copy) % LEAVING
        if slot in leaving:
            leaving.pop(slot).wait_send()
        copy.start()
        leaving[slot] = copy
        return copy

    def drain():
        while leaving:
            leaving.pop(next(iter(leaving))).wait_send()

    def at(start, size):
        return pl.ds(pl.multiple_of(start, 16), size)

    def piece(j, base=0):
        return pl.ds(base + j * part, part)

    pieces = range(PARTS)
    halves = range(CUTS)
    both = [(j, h) for j in pieces for h in halves]

    def project(t, chip, which, out, to, ready=False):
        left = x[t, at((2 * chip + which) * q, q), :]
        for h in halves:
            if not ready:
                loads[f"w{t}{h}"].wait()
            out[h] = mm(left, w[t, h]).astype(to)

    first = [[None, None], [None, None]]
    for t in range(2):
        loads[f"x{t}"].wait()
        project(t, 1 - lo, 1 - k, psend.at[t, 0], BF16)
        if t == 0:
            pl.semaphore_wait(barrier, len(peers))
        first[t][0] = send(message(psend.at[t, 0], precv.at[t, 0], core))
    for t in range(2):
        project(t, 1 - lo, k, pown.at[t, 0], F32, True)
    project(0, lo, 1 - k, psend.at[0, 1], BF16, True)
    first[0][1] = send(message(psend.at[0, 1], precv.at[0, 1], core))

    second = [[], []]

    def over_y(t):
        first[t][0].wait_recv()
        for j in pieces:
            here = piece(j)
            second[t].append([])
            for h in halves:
                own = pown[t, 0, h, here] + precv[t, 0, h, here].astype(F32)
                ysend[t, h, here] = own.astype(BF16)
                copy = message(ysend.at[t, h, here], yrecv.at[t, h, here], near)
                second[t][j].append(send(copy))

    over_y(0)
    over_y(1)
    project(1, lo, 1 - k, psend.at[1, 1], BF16, True)
    first[1][1] = send(message(psend.at[1, 1], precv.at[1, 1], core))
    for t in range(2):
        project(t, lo, k, pown.at[t, 1], F32, True)

    def normalise(t, j, out, to):
        here = piece(j)
        for copy in second[t][j]:
            copy.wait_recv()
        raw = [
            pown[t, 1, h, here] + precv[t, 1, h, here].astype(F32) + yrecv[t, h, here].astype(F32)
            for h in halves
        ]
        squares = sum(jnp.sum(r * r, axis=1, keepdims=True) for r in raw)
        size = jnp.sqrt(squares + norm_eps)
        radius[t, here] = jnp.broadcast_to(size, (part, radius.shape[2]))
        for h in halves:
            value = raw[h] / size
            unit[t, h, here] = value
            out[h, at(to, part)] = value.astype(BF16)

    def visit(s, j):
        return [
            message(a.at[h, piece(j, s * q)], a.at[h, piece(j, (s + 1) * q)], up) for h in halves
        ]

    def text(into, j, target, size, skip, block, h):
        return message(
            b.at[h, at(block * rows + j * q + skip, size)],
            b.at[h, at(into * rows + j * q + skip, size)],
            target,
        )

    def text_core(block, j):
        return [send(text(block, j, core, q, 0, block, h)) for h in halves]

    def go_on(s, j):
        for done, copy in zip(hops[s - 1][j], hops[s][j]):
            done.wait_recv()
            send(copy)

    hops = [[visit(s, j) for j in pieces] for s in range(VISITS - 1)]
    first[0][1].wait_recv()
    for j in pieces:
        normalise(0, j, a, j * part)
        for hop in hops[0][j]:
            send(hop)

    first[1][1].wait_recv()
    across, beside, relay, in_chip = [], [], [], []
    for j in pieces:
        normalise(1, j, b, m * q + j * part)
        across.append([send(text(1, m, prev, part, j * part, 0, h)) for h in halves])
        beside.append([send(text(0, m, near, part, j * part, 0, h)) for h in halves])
        go_on(1, j)
    in_chip += text_core(0, m)
    for j in pieces:
        for h, copy in zip(halves, across[j]):
            copy.wait_recv()
            relay.append(send(text(1, mq, near, part, j * part, 1, h)))
        go_on(2, j)
    in_chip += text_core(1, mq)
    for copy in sum(beside, []):
        copy.wait_recv()
    in_chip += text_core(0, mq)

    for name in "ptb":
        loads[name].wait()
    temperature = jnp.exp(jnp.full((q, 2 * rows), scale_ref[0], F32))
    shift = shift_ref[0]
    named = (
        lax.broadcasted_iota(jnp.int32, (2 * rows, rows), 0) == partner_ref[...]
    ).astype(BF16)
    own = (
        lax.broadcasted_iota(jnp.int32, (q, rows), 1)
        == lax.broadcasted_iota(jnp.int32, (q, rows), 0) + m * q
    )
    positive = mm(own.astype(BF16), named, NT) > 0.5
    drain()

    for (j, h), copy in zip(both, relay):
        copy.wait_recv()
        in_chip.append(send(text(1, m, core, part, j * part, 1, h)))
    for copy in sum(hops[2], []):
        copy.wait_recv()
    for copy in in_chip:
        copy.wait_recv()

    losses = {}
    last = VISITS - 1

    def score(s, scores):
        logits = temperature * scores + shift
        z = jnp.where(positive, -logits, logits) if s == 0 else logits
        u = jnp.exp(-jnp.abs(z))
        soft = jnp.maximum(z, 0.0) + jnp.log1p(u)
        sig = jnp.where(z >= 0.0, 1.0, u) / (1.0 + u)
        grade = temperature * sig
        if s == 0:
            grade = jnp.where(positive, -grade, grade)
        slope[s * q:(s + 1) * q] = grade.astype(BF16)
        slope_t[:, s * q:(s + 1) * q] = grade.T.astype(BF16)
        losses[s] = jnp.sum(soft, axis=1, keepdims=True)

    scores = sum(mm(a[h], b[h], NT) for h in halves)
    score(last, scores[last * q:])

    far = slope[last * q:]
    for h in halves:
        rsend[last - 1, h] = mm(far, b[h]).astype(BF16)

    def homeward(s, j, h):
        return message(rsend.at[s - 1, h, piece(j)], rrecv.at[s - 1, h, piece(j)], down[0])

    ways = {s: [[homeward(s, j, h) for h in halves] for j in pieces] for s in range(1, VISITS)}
    for way in sum(ways[last], []):
        send(way)
    for s in range(last):
        score(s, scores[s * q:(s + 1) * q])

    def text_side(block, which):
        return jnp.concatenate(
            [slope_t[at((2 * block + half) * 2 * q + which * q, q)] for half in range(2)], axis=0
        )

    swap = {}
    for block in (1, 0):
        left = text_side(block, 1 - k)
        for h in halves:
            dbsend[block, h] = mm(left, a[h]).astype(BF16)
        swap[block] = send(message(dbsend.at[block], dbrecv.at[block], core))
    for block in (1, 0):
        left = text_side(block, k)
        for h in halves:
            dbown[block, h] = mm(left, a[h])

    def chip_sum(block, half, j, h):
        where = at(half * q + j * part, part)
        return dbown[block, h, where] + dbrecv[block, h, where].astype(F32)

    skew, beside0, over = [], [], []

    def parcel(block, half, j, held, into, target):
        copies = []
        for h in halves:
            held[h, piece(j)] = chip_sum(block, half, j, h).astype(BF16)
            copies.append(send(message(held.at[h, piece(j)], into.at[h, piece(j)], target)))
        return copies

    swap[1].wait_recv()
    for j in pieces:
        skew.append(parcel(1, lo, j, y1send, y1recv, after_same))
        over.append(parcel(1, 1 - lo, j, xsend, xrecv, after))
    swap[0].wait_recv()
    for j in pieces:
        beside0.append(parcel(0, 1 - lo, j, y0send, y0recv, near))
    for h in halves:
        da[h] = mm(slope[:last * q], b[h])

    def add_way(s, j, h):
        return da[h, piece(j, s * q)] + rrecv[s, h, piece(j)].astype(F32)

    def onward(s, j):
        for h, came, copy in zip(halves, ways[s + 1][j], ways[s][j]):
            came.wait_recv()
            rsend[s - 1, h, piece(j)] = add_way(s, j, h).astype(BF16)
            send(copy)

    spread = (
        lax.broadcasted_iota(jnp.int32, (q, lsend.shape[2]), 1)
        == lax.broadcasted_iota(jnp.int32, (q, lsend.shape[2]), 0) + m * q
    )

    def as_lanes(column):
        line = jnp.sum(jnp.where(spread, column, 0.0), axis=0, keepdims=True)
        return jnp.broadcast_to(line, lsend.shape[1:])

    for j in pieces:
        onward(2, j)
    home = []
    for s in range(1, VISITS):
        lsend[s - 1] = as_lanes(losses[s])
        home.append(send(message(lsend.at[s - 1], lrecv.at[s - 1], down[s - 1])))
    def tangent(t, step, j):
        here = piece(j)
        vec = [unit[t, h, here] for h in halves]
        radial = sum(jnp.sum(vec[h] * step[h], axis=1, keepdims=True) for h in halves)
        size = radius[t, here, 0:1]
        for h in halves:
            moved = (step[h] - vec[h] * radial) / size
            delta[t, h, at(m * q + j * part, part)] = moved.astype(BF16)
            beyond[t].append(send(gather(t, m, near, part, j * part, h)))

    def gather(t, j, target, size, skip, h):
        where = at(j * q + skip, size)
        return message(delta.at[t, h, where], delta.at[t, h, where], target)

    def gather_core(t):
        return [send(gather(t, m, core, q, 0, h)) for h in halves]

    beyond = [[], []]
    inside = [[], []]

    def text_step(j):
        here = piece(j)
        for copy in skew[j] + over[j] + beside0[j]:
            copy.wait_recv()
        tangent(1, [
            chip_sum(0, lo, j, h) + y0recv[h, here].astype(F32)
            + (xrecv[h, here].astype(F32) + y1recv[h, here].astype(F32))
            for h in halves
        ], j)

    def image_step(j):
        for copy in ways[1][j]:
            copy.wait_recv()
        tangent(0, [add_way(0, j, h) for h in halves], j)

    for j in pieces:
        onward(1, j)
        text_step(j)
    inside[1] += gather_core(1)

    total = as_lanes(losses[0])
    for s in range(1, VISITS):
        home[s - 1].wait_recv()
        total = total + lrecv[s - 1]
    lstage[0] = total
    pair = send(message(lstage.at[0], lpeer.at[0], core))

    for j in pieces:
        image_step(j)
    inside[0] += gather_core(0)

    pair.wait_recv()
    lstage[1] = lstage[0] + lpeer[0]
    pair = send(message(lstage.at[1], lpeer.at[1], near))
    drain()

    def result(t, out, chip):
        where = at(chip * 2 * q, 2 * q)
        out[where] = sum(mm(delta[t, h, where], w[t, h], NT) for h in halves).astype(BF16)

    for t in (1, 0):
        for copy in inside[t]:
            copy.wait_recv()
    for (j, h), copy in zip(both, beyond[1]):
        copy.wait_recv()
        inside[1].append(send(gather(1, mq, core, part, j * part, h)))
    result(1, gt_ref, lo)
    result(0, gi_ref, lo)
    for (j, h), copy in zip(both, beyond[0]):
        copy.wait_recv()
        inside[0].append(send(gather(0, mq, core, part, j * part, h)))
    pair.wait_recv()
    loss = (lstage[1] + lpeer[1]) * (1.0 / (STEPS * rows))
    loss_ref[...] = loss[0, 0:rows]
    stores = []

    def put(src, dst):
        copy = pltpu.make_async_copy(src, dst, out_sem.at[len(stores)])
        copy.start()
        stores.append(copy)

    put(loss_ref, loss_hbm)
    for t, out, out_hbm in ((1, gt_ref, gt_hbm), (0, gi_ref, gi_hbm)):
        for copy in inside[t][CUTS:]:
            copy.wait_recv()
        result(t, out, 1 - lo)
        put(out, out_hbm)
    drain()
    for copy in stores:
        copy.wait()


def store(gi, gt, loss, gi_out, gt_out, loss_out, gi_held, gt_held, loss_held, sem):
    held = (gi_held, gt_held, loss_held)
    ins = [pltpu.make_async_copy(s, d, sem.at[i]) for i, (s, d) in enumerate(zip((gi, gt, loss), held))]
    outs = [
        pltpu.make_async_copy(s, d, sem.at[3 + i])
        for i, (s, d) in enumerate(zip(held, (gi_out, gt_out, loss_out)))
    ]
    for copy in ins:
        copy.start()
    for into, out in zip(ins, outs):
        into.wait()
        out.start()
    for out in outs:
        out.wait()


def shards(n, xi, xt, wi, wt, scale, shift, partner):
    rows, share = xi.shape
    wide = wi.shape[1] // CUTS
    q = rows // 4
    vm = pltpu.VMEM
    lanes = -(-rows // 128) * 128
    gi, gt, loss = pl.pallas_call(
        functools.partial(kernel, n),
        out_shape=(
            jax.ShapeDtypeStruct((rows, share), BF16),
            jax.ShapeDtypeStruct((rows, share), BF16),
            jax.ShapeDtypeStruct((rows,), F32),
        ),
        in_specs=[pl.BlockSpec(memory_space=pl.ANY)] * 7,
        out_specs=(pl.BlockSpec(memory_space=pl.ANY),) * 3,
        scratch_shapes=[
            vm((rows, share), BF16),
            vm((rows, share), BF16),
            vm((rows,), F32),
            vm((2, rows, share), BF16),
            vm((2, CUTS, share, wide), BF16),
            vm((1, rows), jnp.int32),
            pltpu.SMEM((1,), F32),
            pltpu.SMEM((1,), F32),
            vm((2, 2, CUTS, q, wide), BF16),
            vm((2, 2, CUTS, q, wide), F32),
            vm((2, 2, CUTS, q, wide), BF16),
            vm((2, CUTS, q, wide), BF16),
            vm((2, CUTS, q, wide), BF16),
            vm((2, CUTS, q, wide), F32),
            vm((2, q, 128), F32),
            vm((CUTS, VISITS * q, wide), BF16),
            vm((CUTS, 2 * rows, wide), BF16),
            vm((VISITS * q, 2 * rows), BF16),
            vm((2 * rows, VISITS * q), BF16),
            vm((CUTS, (VISITS - 1) * q, wide), F32),
            vm((VISITS - 1, CUTS, q, wide), BF16),
            vm((VISITS - 1, CUTS, q, wide), BF16),
            vm((2, CUTS, 2 * q, wide), BF16),
            vm((2, CUTS, 2 * q, wide), F32),
            vm((2, CUTS, 2 * q, wide), BF16),
            vm((CUTS, q, wide), BF16),
            vm((CUTS, q, wide), BF16),
            vm((CUTS, q, wide), BF16),
            vm((CUTS, q, wide), BF16),
            vm((CUTS, q, wide), BF16),
            vm((CUTS, q, wide), BF16),
            vm((2, CUTS, rows, wide), BF16),
            vm((VISITS - 1, 8, lanes), F32),
            vm((VISITS - 1, 8, lanes), F32),
            vm((2, 8, lanes), F32),
            vm((2, 8, lanes), F32),
            pltpu.SemaphoreType.DMA((5 + 2 * CUTS,)),
            pltpu.SemaphoreType.DMA((3,)),
            pltpu.SemaphoreType.DMA((LEAVING,)),
            pltpu.SemaphoreType.DMA((MESSAGES,)),
        ],
        compiler_params=pltpu.CompilerParams(
            collective_id=0, has_side_effects=True, vmem_limit_bytes=62 * 2**20
        ),
    )(xi, xt, wi, wt, scale, shift, partner)
    return pl.pallas_call(
        store,
        out_shape=(
            jax.ShapeDtypeStruct((rows, share), BF16),
            jax.ShapeDtypeStruct((rows, share), BF16),
            jax.ShapeDtypeStruct((rows,), F32),
        ),
        in_specs=[pl.BlockSpec(memory_space=pl.ANY)] * 3,
        out_specs=(pl.BlockSpec(memory_space=pl.ANY),) * 3,
        scratch_shapes=[vm((rows, share), BF16), vm((rows, share), BF16), vm((rows,), F32), pltpu.SemaphoreType.DMA((6,))],
        compiler_params=pltpu.CompilerParams(vmem_limit_bytes=62 * 2**20),
    )(gi, gt, loss)


def solution(mesh):
    placed = (P("dp", "mp"), P("dp", "mp"), P("mp", None), P("mp", None), P(), P(), P("dp", None))
    return jax.shard_map(
        functools.partial(shards, mesh.shape["dp"]),
        mesh=mesh,
        in_specs=placed,
        out_specs=(P("dp", "mp"), P("dp", "mp"), P("dp")),
        check_vma=False,
    )
```

```python
import functools

import jax
import jax.numpy as jnp
from jax import lax
from jax.experimental import pallas as pl
from jax.experimental.pallas import tpu as pltpu
from jax.sharding import PartitionSpec as P

MESH = pl.DeviceIdType.MESH
STEPS = 8
VISITS = STEPS // 2
TICKETS = 54
LEAVING = 24
PARTS = 3
CUTS = 1

norm_eps = 1e-06
F32 = jnp.float32
BF16 = jnp.bfloat16

NN = (((1,), (0,)), ((), ()))
NT = (((1,), (1,)), ((), ()))


def mm(a, b, dims=NN):
    return lax.dot_general(a, b, dims, preferred_element_type=F32)


def kernel(
    n,
    xi_hbm, xt_hbm, wi_hbm, wt_hbm, scale_hbm, shift_hbm, partner_hbm,
    gi_hbm, gt_hbm, loss_hbm,
    gi_ref, gt_ref, loss_ref, x, w, partner_ref, scale_ref, shift_ref, psend, pown, precv, ysend, yrecv, unit, radius,
    a, b, slope, slope_t, da, rsend, rrecv,
    dbsend, dbown, dbrecv, y1send, y1recv, y0send, y0recv, xsend, xrecv,
    delta, lsend, lrecv, lstage, lpeer,
    load_sem, out_sem, ss, rs,
):
    c = lax.axis_index("dp")
    m = lax.axis_index("mp")
    lo, k = m // 2, m % 2
    mq = (m + 2) % 4
    q = a.shape[1] // VISITS
    rows = 4 * q
    wide = w.shape[3]
    part = q // PARTS

    core = (c, m + 1 - 2 * k)
    near = (c, mq)
    prev = ((c + n - 1) % n, mq)
    after = ((c + 1) % n, mq)
    prev_same = ((c + n - 1) % n, m)
    after_same = ((c + 1) % n, m)
    up = ((c + 2) % n, m)
    down = [((c + n - 2 * s) % n, m) for s in range(1, VISITS)]

    loads = {}
    for i, (name, src, dst) in enumerate(
        [("x0", xi_hbm, x.at[0])]
        + [(f"w0{h}", wi_hbm.at[:, pl.ds(h * wide, wide)], w.at[0, h]) for h in range(CUTS)]
        + [("x1", xt_hbm, x.at[1])]
        + [(f"w1{h}", wt_hbm.at[:, pl.ds(h * wide, wide)], w.at[1, h]) for h in range(CUTS)]
        + [("p", partner_hbm, partner_ref), ("t", scale_hbm, scale_ref), ("b", shift_hbm, shift_ref)]
    ):
        loads[name] = pltpu.make_async_copy(src, dst, load_sem.at[i])
        loads[name].start()

    barrier = pltpu.get_barrier_semaphore()
    peers = [core, near, prev, after, prev_same, after_same, up, down[0]]
    for peer in peers:
        pl.semaphore_signal(barrier, inc=1, device_id=peer, device_id_type=MESH)

    slots = {}
    leaving = {}
    taken = [0]

    def ticket():
        taken[0] += 1
        return taken[0] - 1

    def message(src, dst, target, shared=None):
        i = len(slots)
        copy = pltpu.make_async_remote_copy(
            src_ref=src, dst_ref=dst, send_sem=ss.at[i % LEAVING],
            recv_sem=rs.at[ticket() if shared is None else shared],
            device_id=target, device_id_type=MESH,
        )
        slots[i] = copy
        return copy

    def send(copy):
        slot = next(i for i, other in slots.items() if other is copy) % LEAVING
        if slot in leaving:
            leaving.pop(slot).wait_send()
        copy.start()
        leaving[slot] = copy
        return copy

    def drain():
        while leaving:
            leaving.pop(next(iter(leaving))).wait_send()

    def arrival(ref, shared):
        pltpu.make_async_remote_copy(
            src_ref=ref, dst_ref=ref, send_sem=ss.at[0], recv_sem=rs.at[shared],
            device_id=core, device_id_type=MESH,
        ).wait_recv()

    def at(start, size):
        return pl.ds(pl.multiple_of(start, 16), size)

    def piece(j, base=0):
        return pl.ds(base + j * part, part)

    pieces = range(PARTS)
    halves = range(CUTS)
    both = [(j, h) for j in pieces for h in halves]

    def project(t, chip, which, out, to, ready=False):
        left = x[t, at((2 * chip + which) * q, q), :]
        for h in halves:
            if not ready:
                loads[f"w{t}{h}"].wait()
            out[h] = mm(left, w[t, h]).astype(to)

    first = [[None, None], [None, None]]
    for t in range(2):
        loads[f"x{t}"].wait()
        project(t, 1 - lo, 1 - k, psend.at[t, 0], BF16)
        if t == 0:
            pl.semaphore_wait(barrier, len(peers))
        first[t][0] = send(message(psend.at[t, 0], precv.at[t, 0], core))
    for t in range(2):
        project(t, 1 - lo, k, pown.at[t, 0], F32, True)
    project(0, lo, 1 - k, psend.at[0, 1], BF16, True)
    first[0][1] = send(message(psend.at[0, 1], precv.at[0, 1], core))

    second = [[], []]

    def over_y(t):
        first[t][0].wait_recv()
        for j in pieces:
            here = piece(j)
            second[t].append([])
            for h in halves:
                own = pown[t, 0, h, here] + precv[t, 0, h, here].astype(F32)
                ysend[t, h, here] = own.astype(BF16)
                copy = message(ysend.at[t, h, here], yrecv.at[t, h, here], near)
                second[t][j].append(send(copy))

    over_y(0)
    over_y(1)
    project(1, lo, 1 - k, psend.at[1, 1], BF16, True)
    first[1][1] = send(message(psend.at[1, 1], precv.at[1, 1], core))
    for t in range(2):
        project(t, lo, k, pown.at[t, 1], F32, True)

    def normalise(t, j, out, to):
        here = piece(j)
        for copy in second[t][j]:
            copy.wait_recv()
        raw = [
            pown[t, 1, h, here] + precv[t, 1, h, here].astype(F32) + yrecv[t, h, here].astype(F32)
            for h in halves
        ]
        squares = sum(jnp.sum(r * r, axis=1, keepdims=True) for r in raw)
        size = jnp.sqrt(squares + norm_eps)
        radius[t, here] = jnp.broadcast_to(size, (part, radius.shape[2]))
        for h in halves:
            value = raw[h] / size
            unit[t, h, here] = value
            out[h, at(to, part)] = value.astype(BF16)

    final = ticket()

    def visit(s, j):
        shared = final if s == VISITS - 2 else None
        return [
            message(a.at[h, piece(j, s * q)], a.at[h, piece(j, (s + 1) * q)], up, shared)
            for h in halves
        ]

    in_chip, beside = ticket(), ticket()

    def text(into, j, target, size, skip, block, h, shared=None):
        return message(
            b.at[h, at(block * rows + j * q + skip, size)],
            b.at[h, at(into * rows + j * q + skip, size)],
            target, shared,
        )

    def text_core(block, j):
        for h in halves:
            send(text(block, j, core, q, 0, block, h, in_chip))

    def go_on(s, j):
        for done, copy in zip(hops[s - 1][j], hops[s][j]):
            done.wait_recv()
            send(copy)

    hops = [[visit(s, j) for j in pieces] for s in range(VISITS - 1)]
    first[0][1].wait_recv()
    for j in pieces:
        normalise(0, j, a, j * part)
        for hop in hops[0][j]:
            send(hop)

    first[1][1].wait_recv()
    across, relay = [], []
    for j in pieces:
        normalise(1, j, b, m * q + j * part)
        across.append([send(text(1, m, prev, part, j * part, 0, h)) for h in halves])
        for h in halves:
            send(text(0, m, near, part, j * part, 0, h, beside))
        go_on(1, j)
    text_core(0, m)
    for j in pieces:
        for h, copy in zip(halves, across[j]):
            copy.wait_recv()
            relay.append(send(text(1, mq, near, part, j * part, 1, h)))
        go_on(2, j)
    text_core(1, mq)
    arrival(b.at[:, at(mq * q, q)], beside)
    text_core(0, mq)

    for name in "ptb":
        loads[name].wait()
    temperature = jnp.exp(jnp.full((q, 2 * rows), scale_ref[0], F32))
    shift = shift_ref[0]
    named = (
        lax.broadcasted_iota(jnp.int32, (2 * rows, rows), 0) == partner_ref[...]
    ).astype(BF16)
    own = (
        lax.broadcasted_iota(jnp.int32, (q, rows), 1)
        == lax.broadcasted_iota(jnp.int32, (q, rows), 0) + m * q
    )
    positive = mm(own.astype(BF16), named, NT) > 0.5
    drain()

    for (j, h), copy in zip(both, relay):
        copy.wait_recv()
        send(text(1, m, core, part, j * part, 1, h, in_chip))
    arrival(a.at[:, pl.ds((VISITS - 1) * q, q)], final)
    arrival(b.at[:, pl.ds(0, 4 * q)], in_chip)

    losses = {}
    last = VISITS - 1

    def score(s, scores):
        logits = temperature * scores + shift
        z = jnp.where(positive, -logits, logits) if s == 0 else logits
        u = jnp.exp(-jnp.abs(z))
        soft = jnp.maximum(z, 0.0) + jnp.log1p(u)
        sig = jnp.where(z >= 0.0, 1.0, u) / (1.0 + u)
        grade = temperature * sig
        if s == 0:
            grade = jnp.where(positive, -grade, grade)
        slope[s * q:(s + 1) * q] = grade.astype(BF16)
        slope_t[:, s * q:(s + 1) * q] = grade.T.astype(BF16)
        losses[s] = jnp.sum(soft, axis=1, keepdims=True)

    scores = sum(mm(a[h], b[h], NT) for h in halves)
    score(last, scores[last * q:])

    far = slope[last * q:]
    for h in halves:
        rsend[last - 1, h] = mm(far, b[h]).astype(BF16)

    def homeward(s, j, h):
        return message(rsend.at[s - 1, h, piece(j)], rrecv.at[s - 1, h, piece(j)], down[0])

    ways = {s: [[homeward(s, j, h) for h in halves] for j in pieces] for s in range(1, VISITS)}
    for way in sum(ways[last], []):
        send(way)
    for s in range(last):
        score(s, scores[s * q:(s + 1) * q])

    def text_side(block, which):
        return jnp.concatenate(
            [slope_t[at((2 * block + half) * 2 * q + which * q, q)] for half in range(2)], axis=0
        )

    swap = {}
    for block in (1, 0):
        left = text_side(block, 1 - k)
        for h in halves:
            dbsend[block, h] = mm(left, a[h]).astype(BF16)
        swap[block] = send(message(dbsend.at[block], dbrecv.at[block], core))
    for block in (1, 0):
        left = text_side(block, k)
        for h in halves:
            dbown[block, h] = mm(left, a[h])

    def chip_sum(block, half, j, h):
        where = at(half * q + j * part, part)
        return dbown[block, h, where] + dbrecv[block, h, where].astype(F32)

    shares = [ticket() for _ in pieces]

    def parcel(block, half, j, held, into, target):
        for h in halves:
            held[h, piece(j)] = chip_sum(block, half, j, h).astype(BF16)
            send(message(held.at[h, piece(j)], into.at[h, piece(j)], target, shares[j]))

    swap[1].wait_recv()
    for j in pieces:
        parcel(1, lo, j, y1send, y1recv, after_same)
        parcel(1, 1 - lo, j, xsend, xrecv, after)
    swap[0].wait_recv()
    for j in pieces:
        parcel(0, 1 - lo, j, y0send, y0recv, near)
    for h in halves:
        da[h] = mm(slope[:last * q], b[h])

    def add_way(s, j, h):
        return da[h, piece(j, s * q)] + rrecv[s, h, piece(j)].astype(F32)

    def onward(s, j):
        for h, came, copy in zip(halves, ways[s + 1][j], ways[s][j]):
            came.wait_recv()
            rsend[s - 1, h, piece(j)] = add_way(s, j, h).astype(BF16)
            send(copy)

    spread = (
        lax.broadcasted_iota(jnp.int32, (q, lsend.shape[2]), 1)
        == lax.broadcasted_iota(jnp.int32, (q, lsend.shape[2]), 0) + m * q
    )

    def as_lanes(column):
        line = jnp.sum(jnp.where(spread, column, 0.0), axis=0, keepdims=True)
        return jnp.broadcast_to(line, lsend.shape[1:])

    for j in pieces:
        onward(2, j)
    home = []
    for s in range(1, VISITS):
        lsend[s - 1] = as_lanes(losses[s])
        home.append(send(message(lsend.at[s - 1], lrecv.at[s - 1], down[s - 1])))
    def tangent(t, step, j):
        here = piece(j)
        vec = [unit[t, h, here] for h in halves]
        radial = sum(jnp.sum(vec[h] * step[h], axis=1, keepdims=True) for h in halves)
        size = radius[t, here, 0:1]
        for h in halves:
            moved = (step[h] - vec[h] * radial) / size
            delta[t, h, at(m * q + j * part, part)] = moved.astype(BF16)
            beyond[t].append(send(gather(t, m, near, part, j * part, h)))

    handed = [ticket(), ticket()]

    def gather(t, j, target, size, skip, h, shared=None):
        where = at(j * q + skip, size)
        return message(delta.at[t, h, where], delta.at[t, h, where], target, shared)

    def gather_core(t):
        return [send(gather(t, m, core, q, 0, h)) for h in halves]

    beyond = [[], []]
    inside = [[], []]

    def text_step(j):
        here = piece(j)
        arrival(y1recv.at[:, pl.ds(0, 3 * part)], shares[j])
        tangent(1, [
            chip_sum(0, lo, j, h) + y0recv[h, here].astype(F32)
            + (xrecv[h, here].astype(F32) + y1recv[h, here].astype(F32))
            for h in halves
        ], j)

    def image_step(j):
        for copy in ways[1][j]:
            copy.wait_recv()
        tangent(0, [add_way(0, j, h) for h in halves], j)

    for j in pieces:
        onward(1, j)
        text_step(j)
    inside[1] += gather_core(1)

    total = as_lanes(losses[0])
    for s in range(1, VISITS):
        home[s - 1].wait_recv()
        total = total + lrecv[s - 1]
    lstage[0] = total
    pair = send(message(lstage.at[0], lpeer.at[0], core))

    for j in pieces:
        image_step(j)
    inside[0] += gather_core(0)

    pair.wait_recv()
    lstage[1] = lstage[0] + lpeer[0]
    pair = send(message(lstage.at[1], lpeer.at[1], near))
    drain()

    def result(t, out, chip):
        where = at(chip * 2 * q, 2 * q)
        out[where] = sum(mm(delta[t, h, where], w[t, h], NT) for h in halves).astype(BF16)

    for t in (1, 0):
        for copy in inside[t]:
            copy.wait_recv()
    for (j, h), copy in zip(both, beyond[1]):
        copy.wait_recv()
        send(gather(1, mq, core, part, j * part, h, handed[1]))
    result(1, gt_ref, lo)
    result(0, gi_ref, lo)
    for (j, h), copy in zip(both, beyond[0]):
        copy.wait_recv()
        send(gather(0, mq, core, part, j * part, h, handed[0]))
    pair.wait_recv()
    loss = (lstage[1] + lpeer[1]) * (1.0 / (STEPS * rows))
    loss_ref[...] = loss[0, 0:rows]
    stores = []

    def put(src, dst):
        copy = pltpu.make_async_copy(src, dst, out_sem.at[len(stores)])
        copy.start()
        stores.append(copy)

    put(loss_ref, loss_hbm)
    for t, out, out_hbm in ((1, gt_ref, gt_hbm), (0, gi_ref, gi_hbm)):
        arrival(delta.at[t, :, at((m + 3 - 2 * k) % 4 * q, q)], handed[t])
        result(t, out, 1 - lo)
        put(out, out_hbm)
    drain()
    for copy in stores:
        copy.wait()


def store(gi, gt, loss, gi_out, gt_out, loss_out, gi_held, gt_held, loss_held, sem):
    held = (gi_held, gt_held, loss_held)
    ins = [pltpu.make_async_copy(s, d, sem.at[i]) for i, (s, d) in enumerate(zip((gi, gt, loss), held))]
    outs = [
        pltpu.make_async_copy(s, d, sem.at[3 + i])
        for i, (s, d) in enumerate(zip(held, (gi_out, gt_out, loss_out)))
    ]
    for copy in ins:
        copy.start()
    for into, out in zip(ins, outs):
        into.wait()
        out.start()
    for out in outs:
        out.wait()


def shards(n, xi, xt, wi, wt, scale, shift, partner):
    rows, share = xi.shape
    wide = wi.shape[1] // CUTS
    q = rows // 4
    vm = pltpu.VMEM
    lanes = -(-rows // 128) * 128
    gi, gt, loss = pl.pallas_call(
        functools.partial(kernel, n),
        out_shape=(
            jax.ShapeDtypeStruct((rows, share), BF16),
            jax.ShapeDtypeStruct((rows, share), BF16),
            jax.ShapeDtypeStruct((rows,), F32),
        ),
        in_specs=[pl.BlockSpec(memory_space=pl.ANY)] * 7,
        out_specs=(pl.BlockSpec(memory_space=pl.ANY),) * 3,
        scratch_shapes=[
            vm((rows, share), BF16),
            vm((rows, share), BF16),
            vm((rows,), F32),
            vm((2, rows, share), BF16),
            vm((2, CUTS, share, wide), BF16),
            vm((1, rows), jnp.int32),
            pltpu.SMEM((1,), F32),
            pltpu.SMEM((1,), F32),
            vm((2, 2, CUTS, q, wide), BF16),
            vm((2, 2, CUTS, q, wide), F32),
            vm((2, 2, CUTS, q, wide), BF16),
            vm((2, CUTS, q, wide), BF16),
            vm((2, CUTS, q, wide), BF16),
            vm((2, CUTS, q, wide), F32),
            vm((2, q, 128), F32),
            vm((CUTS, VISITS * q, wide), BF16),
            vm((CUTS, 2 * rows, wide), BF16),
            vm((VISITS * q, 2 * rows), BF16),
            vm((2 * rows, VISITS * q), BF16),
            vm((CUTS, (VISITS - 1) * q, wide), F32),
            vm((VISITS - 1, CUTS, q, wide), BF16),
            vm((VISITS - 1, CUTS, q, wide), BF16),
            vm((2, CUTS, 2 * q, wide), BF16),
            vm((2, CUTS, 2 * q, wide), F32),
            vm((2, CUTS, 2 * q, wide), BF16),
            vm((CUTS, q, wide), BF16),
            vm((CUTS, q, wide), BF16),
            vm((CUTS, q, wide), BF16),
            vm((CUTS, q, wide), BF16),
            vm((CUTS, q, wide), BF16),
            vm((CUTS, q, wide), BF16),
            vm((2, CUTS, rows, wide), BF16),
            vm((VISITS - 1, 8, lanes), F32),
            vm((VISITS - 1, 8, lanes), F32),
            vm((2, 8, lanes), F32),
            vm((2, 8, lanes), F32),
            pltpu.SemaphoreType.DMA((5 + 2 * CUTS,)),
            pltpu.SemaphoreType.DMA((3,)),
            pltpu.SemaphoreType.DMA((LEAVING,)),
            pltpu.SemaphoreType.DMA((TICKETS,)),
        ],
        compiler_params=pltpu.CompilerParams(
            collective_id=0, has_side_effects=True, vmem_limit_bytes=62 * 2**20
        ),
    )(xi, xt, wi, wt, scale, shift, partner)
    return pl.pallas_call(
        store,
        out_shape=(
            jax.ShapeDtypeStruct((rows, share), BF16),
            jax.ShapeDtypeStruct((rows, share), BF16),
            jax.ShapeDtypeStruct((rows,), F32),
        ),
        in_specs=[pl.BlockSpec(memory_space=pl.ANY)] * 3,
        out_specs=(pl.BlockSpec(memory_space=pl.ANY),) * 3,
        scratch_shapes=[vm((rows, share), BF16), vm((rows, share), BF16), vm((rows,), F32), pltpu.SemaphoreType.DMA((6,))],
        compiler_params=pltpu.CompilerParams(vmem_limit_bytes=62 * 2**20),
    )(gi, gt, loss)


def solution(mesh):
    placed = (P("dp", "mp"), P("dp", "mp"), P("mp", None), P("mp", None), P(), P(), P("dp", None))
    return jax.shard_map(
        functools.partial(shards, mesh.shape["dp"]),
        mesh=mesh,
        in_specs=placed,
        out_specs=(P("dp", "mp"), P("dp", "mp"), P("dp")),
        check_vma=False,
    )
```

```python
import functools

import jax
import jax.numpy as jnp
from jax import lax
from jax.experimental import pallas as pl
from jax.experimental.pallas import tpu as pltpu
from jax.sharding import PartitionSpec as P

MESH = pl.DeviceIdType.MESH
STEPS = 8
VISITS = STEPS // 2
TICKETS = 54
LEAVING = 24
PARTS = 3
CUTS = 1

norm_eps = 1e-06
F32 = jnp.float32
BF16 = jnp.bfloat16

NN = (((1,), (0,)), ((), ()))
NT = (((1,), (1,)), ((), ()))


def mm(a, b, dims=NN):
    return lax.dot_general(a, b, dims, preferred_element_type=F32)


def kernel(
    n,
    xi_hbm, xt_hbm, wi_hbm, wt_hbm, scale_hbm, shift_hbm, partner_hbm,
    gi_hbm, gt_hbm, loss_hbm,
    gi_ref, gt_ref, loss_ref, x, w, partner_ref, scale_ref, shift_ref, psend, pown, precv, ysend, yrecv, unit, radius,
    a, b, slope, slope_t, da, rsend, rrecv,
    dbsend, dbown, dbrecv, y1send, y1recv, y0send, y0recv, xsend, xrecv,
    delta, lsend, lrecv, lstage, lpeer,
    load_sem, out_sem, ss, rs,
):
    c = lax.axis_index("dp")
    m = lax.axis_index("mp")
    lo, k = m // 2, m % 2
    mq = (m + 2) % 4
    q = a.shape[1] // VISITS
    rows = 4 * q
    wide = w.shape[3]
    part = q // PARTS

    core = (c, m + 1 - 2 * k)
    near = (c, mq)
    prev = ((c + n - 1) % n, mq)
    after = ((c + 1) % n, mq)
    after_same = ((c + 1) % n, m)
    up = ((c + 2) % n, m)
    down = [((c + n - 2 * s) % n, m) for s in range(1, VISITS)]

    loads = {}
    for i, (name, src, dst) in enumerate(
        [("x0", xi_hbm, x.at[0])]
        + [(f"w0{h}", wi_hbm.at[:, pl.ds(h * wide, wide)], w.at[0, h]) for h in range(CUTS)]
        + [("x1", xt_hbm, x.at[1])]
        + [(f"w1{h}", wt_hbm.at[:, pl.ds(h * wide, wide)], w.at[1, h]) for h in range(CUTS)]
        + [("p", partner_hbm, partner_ref), ("t", scale_hbm, scale_ref), ("b", shift_hbm, shift_ref)]
    ):
        loads[name] = pltpu.make_async_copy(src, dst, load_sem.at[i])
        loads[name].start()

    barrier = pltpu.get_barrier_semaphore()
    peers = [core, near, after, down[0]]
    for peer in peers:
        pl.semaphore_signal(barrier, inc=1, device_id=peer, device_id_type=MESH)

    slots = {}
    leaving = {}
    taken = [0]

    def ticket():
        taken[0] += 1
        return taken[0] - 1

    def message(src, dst, target, shared=None):
        i = len(slots)
        copy = pltpu.make_async_remote_copy(
            src_ref=src, dst_ref=dst, send_sem=ss.at[i % LEAVING],
            recv_sem=rs.at[ticket() if shared is None else shared],
            device_id=target, device_id_type=MESH,
        )
        slots[i] = copy
        return copy

    def send(copy):
        slot = next(i for i, other in slots.items() if other is copy) % LEAVING
        if slot in leaving:
            leaving.pop(slot).wait_send()
        copy.start()
        leaving[slot] = copy
        return copy

    def drain():
        while leaving:
            leaving.pop(next(iter(leaving))).wait_send()

    def arrival(ref, shared):
        pltpu.make_async_remote_copy(
            src_ref=ref, dst_ref=ref, send_sem=ss.at[0], recv_sem=rs.at[shared],
            device_id=core, device_id_type=MESH,
        ).wait_recv()

    def at(start, size):
        return pl.ds(pl.multiple_of(start, 16), size)

    def piece(j, base=0):
        return pl.ds(base + j * part, part)

    pieces = range(PARTS)
    halves = range(CUTS)
    both = [(j, h) for j in pieces for h in halves]

    def project(t, chip, which, out, to, ready=False):
        left = x[t, at((2 * chip + which) * q, q), :]
        for h in halves:
            if not ready:
                loads[f"w{t}{h}"].wait()
            out[h] = mm(left, w[t, h]).astype(to)

    first = [[None, None], [None, None]]
    for t in range(2):
        loads[f"x{t}"].wait()
        project(t, 1 - lo, 1 - k, psend.at[t, 0], BF16)
        if t == 0:
            pl.semaphore_wait(barrier, len(peers))
        first[t][0] = send(message(psend.at[t, 0], precv.at[t, 0], core))
    for t in range(2):
        project(t, 1 - lo, k, pown.at[t, 0], F32, True)
    project(0, lo, 1 - k, psend.at[0, 1], BF16, True)
    first[0][1] = send(message(psend.at[0, 1], precv.at[0, 1], core))

    second = [[], []]

    def over_y(t):
        first[t][0].wait_recv()
        for j in pieces:
            here = piece(j)
            second[t].append([])
            for h in halves:
                own = pown[t, 0, h, here] + precv[t, 0, h, here].astype(F32)
                ysend[t, h, here] = own.astype(BF16)
                copy = message(ysend.at[t, h, here], yrecv.at[t, h, here], near)
                second[t][j].append(send(copy))

    over_y(0)
    over_y(1)
    project(1, lo, 1 - k, psend.at[1, 1], BF16, True)
    first[1][1] = send(message(psend.at[1, 1], precv.at[1, 1], core))
    for t in range(2):
        project(t, lo, k, pown.at[t, 1], F32, True)

    def normalise(t, j, out, to):
        here = piece(j)
        for copy in second[t][j]:
            copy.wait_recv()
        raw = [
            pown[t, 1, h, here] + precv[t, 1, h, here].astype(F32) + yrecv[t, h, here].astype(F32)
            for h in halves
        ]
        squares = sum(jnp.sum(r * r, axis=1, keepdims=True) for r in raw)
        size = jnp.sqrt(squares + norm_eps)
        radius[t, here] = jnp.broadcast_to(size, (part, radius.shape[2]))
        for h in halves:
            value = raw[h] / size
            unit[t, h, here] = value
            out[h, at(to, part)] = value.astype(BF16)

    final = ticket()

    def visit(s, j):
        shared = final if s == VISITS - 2 else None
        return [
            message(a.at[h, piece(j, s * q)], a.at[h, piece(j, (s + 1) * q)], up, shared)
            for h in halves
        ]

    in_chip, beside = ticket(), ticket()

    def text(into, j, target, size, skip, block, h, shared=None):
        return message(
            b.at[h, at(block * rows + j * q + skip, size)],
            b.at[h, at(into * rows + j * q + skip, size)],
            target, shared,
        )

    def text_core(block, j):
        for h in halves:
            send(text(block, j, core, q, 0, block, h, in_chip))

    def go_on(s, j):
        for done, copy in zip(hops[s - 1][j], hops[s][j]):
            done.wait_recv()
            send(copy)

    hops = [[visit(s, j) for j in pieces] for s in range(VISITS - 1)]
    first[0][1].wait_recv()
    for j in pieces:
        normalise(0, j, a, j * part)
        for hop in hops[0][j]:
            send(hop)

    first[1][1].wait_recv()
    across, relay = [], []
    for j in pieces:
        normalise(1, j, b, m * q + j * part)
        across.append([send(text(1, m, prev, part, j * part, 0, h)) for h in halves])
        for h in halves:
            send(text(0, m, near, part, j * part, 0, h, beside))
        go_on(1, j)
    text_core(0, m)
    for j in pieces:
        for h, copy in zip(halves, across[j]):
            copy.wait_recv()
            relay.append(send(text(1, mq, near, part, j * part, 1, h)))
        go_on(2, j)
    text_core(1, mq)
    arrival(b.at[:, at(mq * q, q)], beside)
    text_core(0, mq)

    for name in "ptb":
        loads[name].wait()
    temperature = jnp.exp(jnp.full((q, 2 * rows), scale_ref[0], F32))
    shift = shift_ref[0]
    named = (
        lax.broadcasted_iota(jnp.int32, (2 * rows, rows), 0) == partner_ref[...]
    ).astype(BF16)
    own = (
        lax.broadcasted_iota(jnp.int32, (q, rows), 1)
        == lax.broadcasted_iota(jnp.int32, (q, rows), 0) + m * q
    )
    positive = mm(own.astype(BF16), named, NT) > 0.5
    drain()

    for (j, h), copy in zip(both, relay):
        copy.wait_recv()
        send(text(1, m, core, part, j * part, 1, h, in_chip))
    arrival(a.at[:, pl.ds((VISITS - 1) * q, q)], final)
    arrival(b.at[:, pl.ds(0, 4 * q)], in_chip)

    losses = {}
    last = VISITS - 1

    def score(s, scores):
        logits = temperature * scores + shift
        z = jnp.where(positive, -logits, logits) if s == 0 else logits
        u = jnp.exp(-jnp.abs(z))
        soft = jnp.maximum(z, 0.0) + jnp.log1p(u)
        sig = jnp.where(z >= 0.0, 1.0, u) / (1.0 + u)
        grade = temperature * sig
        if s == 0:
            grade = jnp.where(positive, -grade, grade)
        slope[s * q:(s + 1) * q] = grade.astype(BF16)
        slope_t[:, s * q:(s + 1) * q] = grade.T.astype(BF16)
        losses[s] = jnp.sum(soft, axis=1, keepdims=True)

    scores = sum(mm(a[h], b[h], NT) for h in halves)
    score(last, scores[last * q:])

    far = slope[last * q:]
    for h in halves:
        rsend[last - 1, h] = mm(far, b[h]).astype(BF16)

    def homeward(s, j, h):
        return message(rsend.at[s - 1, h, piece(j)], rrecv.at[s - 1, h, piece(j)], down[0])

    ways = {s: [[homeward(s, j, h) for h in halves] for j in pieces] for s in range(1, VISITS)}
    for way in sum(ways[last], []):
        send(way)
    for s in range(last):
        score(s, scores[s * q:(s + 1) * q])

    def text_side(block, which):
        return jnp.concatenate(
            [slope_t[at((2 * block + half) * 2 * q + which * q, q)] for half in range(2)], axis=0
        )

    swap = {}
    for block in (1, 0):
        left = text_side(block, 1 - k)
        for h in halves:
            dbsend[block, h] = mm(left, a[h]).astype(BF16)
        swap[block] = send(message(dbsend.at[block], dbrecv.at[block], core))
    for block in (1, 0):
        left = text_side(block, k)
        for h in halves:
            dbown[block, h] = mm(left, a[h])

    def chip_sum(block, half, j, h):
        where = at(half * q + j * part, part)
        return dbown[block, h, where] + dbrecv[block, h, where].astype(F32)

    shares = [ticket() for _ in pieces]

    def parcel(block, half, j, held, into, target):
        for h in halves:
            held[h, piece(j)] = chip_sum(block, half, j, h).astype(BF16)
            send(message(held.at[h, piece(j)], into.at[h, piece(j)], target, shares[j]))

    swap[1].wait_recv()
    for j in pieces:
        parcel(1, lo, j, y1send, y1recv, after_same)
        parcel(1, 1 - lo, j, xsend, xrecv, after)
    swap[0].wait_recv()
    for j in pieces:
        parcel(0, 1 - lo, j, y0send, y0recv, near)
    for h in halves:
        da[h] = mm(slope[:last * q], b[h])

    def add_way(s, j, h):
        return da[h, piece(j, s * q)] + rrecv[s, h, piece(j)].astype(F32)

    def onward(s, j):
        for h, came, copy in zip(halves, ways[s + 1][j], ways[s][j]):
            came.wait_recv()
            rsend[s - 1, h, piece(j)] = add_way(s, j, h).astype(BF16)
            send(copy)

    spread = (
        lax.broadcasted_iota(jnp.int32, (q, lsend.shape[2]), 1)
        == lax.broadcasted_iota(jnp.int32, (q, lsend.shape[2]), 0) + m * q
    )

    def as_lanes(column):
        line = jnp.sum(jnp.where(spread, column, 0.0), axis=0, keepdims=True)
        return jnp.broadcast_to(line, lsend.shape[1:])

    for j in pieces:
        onward(2, j)
    home = []
    for s in range(1, VISITS):
        lsend[s - 1] = as_lanes(losses[s])
        home.append(send(message(lsend.at[s - 1], lrecv.at[s - 1], down[s - 1])))
    def tangent(t, step, j):
        here = piece(j)
        vec = [unit[t, h, here] for h in halves]
        radial = sum(jnp.sum(vec[h] * step[h], axis=1, keepdims=True) for h in halves)
        size = radius[t, here, 0:1]
        for h in halves:
            moved = (step[h] - vec[h] * radial) / size
            delta[t, h, at(m * q + j * part, part)] = moved.astype(BF16)
            beyond[t].append(send(gather(t, m, near, part, j * part, h)))

    handed = [ticket(), ticket()]

    def gather(t, j, target, size, skip, h, shared=None):
        where = at(j * q + skip, size)
        return message(delta.at[t, h, where], delta.at[t, h, where], target, shared)

    def gather_core(t):
        return [send(gather(t, m, core, q, 0, h)) for h in halves]

    beyond = [[], []]
    inside = [[], []]

    def text_step(j):
        here = piece(j)
        arrival(y1recv.at[:, pl.ds(0, 3 * part)], shares[j])
        tangent(1, [
            chip_sum(0, lo, j, h) + y0recv[h, here].astype(F32)
            + (xrecv[h, here].astype(F32) + y1recv[h, here].astype(F32))
            for h in halves
        ], j)

    def image_step(j):
        for copy in ways[1][j]:
            copy.wait_recv()
        tangent(0, [add_way(0, j, h) for h in halves], j)

    for j in pieces:
        onward(1, j)
        text_step(j)
    inside[1] += gather_core(1)

    total = as_lanes(losses[0])
    for s in range(1, VISITS):
        home[s - 1].wait_recv()
        total = total + lrecv[s - 1]
    lstage[0] = total
    pair = send(message(lstage.at[0], lpeer.at[0], core))

    for j in pieces:
        image_step(j)
    inside[0] += gather_core(0)

    pair.wait_recv()
    lstage[1] = lstage[0] + lpeer[0]
    pair = send(message(lstage.at[1], lpeer.at[1], near))
    drain()

    def result(t, out, chip):
        where = at(chip * 2 * q, 2 * q)
        out[where] = sum(mm(delta[t, h, where], w[t, h], NT) for h in halves).astype(BF16)

    for t in (1, 0):
        for copy in inside[t]:
            copy.wait_recv()
    for (j, h), copy in zip(both, beyond[1]):
        copy.wait_recv()
        send(gather(1, mq, core, part, j * part, h, handed[1]))
    result(1, gt_ref, lo)
    result(0, gi_ref, lo)
    for (j, h), copy in zip(both, beyond[0]):
        copy.wait_recv()
        send(gather(0, mq, core, part, j * part, h, handed[0]))
    pair.wait_recv()
    loss = (lstage[1] + lpeer[1]) * (1.0 / (STEPS * rows))
    loss_ref[...] = loss[0, 0:rows]
    stores = []

    def put(src, dst):
        copy = pltpu.make_async_copy(src, dst, out_sem.at[len(stores)])
        copy.start()
        stores.append(copy)

    put(loss_ref, loss_hbm)
    for t, out, out_hbm in ((1, gt_ref, gt_hbm), (0, gi_ref, gi_hbm)):
        arrival(delta.at[t, :, at((m + 3 - 2 * k) % 4 * q, q)], handed[t])
        result(t, out, 1 - lo)
        put(out, out_hbm)
    drain()
    for copy in stores:
        copy.wait()


def store(gi, gt, loss, gi_out, gt_out, loss_out, gi_held, gt_held, loss_held, sem):
    held = (gi_held, gt_held, loss_held)
    ins = [pltpu.make_async_copy(s, d, sem.at[i]) for i, (s, d) in enumerate(zip((gi, gt, loss), held))]
    outs = [
        pltpu.make_async_copy(s, d, sem.at[3 + i])
        for i, (s, d) in enumerate(zip(held, (gi_out, gt_out, loss_out)))
    ]
    for copy in ins:
        copy.start()
    for into, out in zip(ins, outs):
        into.wait()
        out.start()
    for out in outs:
        out.wait()


def shards(n, xi, xt, wi, wt, scale, shift, partner):
    rows, share = xi.shape
    wide = wi.shape[1] // CUTS
    q = rows // 4
    vm = pltpu.VMEM
    lanes = -(-rows // 128) * 128
    gi, gt, loss = pl.pallas_call(
        functools.partial(kernel, n),
        out_shape=(
            jax.ShapeDtypeStruct((rows, share), BF16),
            jax.ShapeDtypeStruct((rows, share), BF16),
            jax.ShapeDtypeStruct((rows,), F32),
        ),
        in_specs=[pl.BlockSpec(memory_space=pl.ANY)] * 7,
        out_specs=(pl.BlockSpec(memory_space=pl.ANY),) * 3,
        scratch_shapes=[
            vm((rows, share), BF16),
            vm((rows, share), BF16),
            vm((rows,), F32),
            vm((2, rows, share), BF16),
            vm((2, CUTS, share, wide), BF16),
            vm((1, rows), jnp.int32),
            pltpu.SMEM((1,), F32),
            pltpu.SMEM((1,), F32),
            vm((2, 2, CUTS, q, wide), BF16),
            vm((2, 2, CUTS, q, wide), F32),
            vm((2, 2, CUTS, q, wide), BF16),
            vm((2, CUTS, q, wide), BF16),
            vm((2, CUTS, q, wide), BF16),
            vm((2, CUTS, q, wide), F32),
            vm((2, q, 128), F32),
            vm((CUTS, VISITS * q, wide), BF16),
            vm((CUTS, 2 * rows, wide), BF16),
            vm((VISITS * q, 2 * rows), BF16),
            vm((2 * rows, VISITS * q), BF16),
            vm((CUTS, (VISITS - 1) * q, wide), F32),
            vm((VISITS - 1, CUTS, q, wide), BF16),
            vm((VISITS - 1, CUTS, q, wide), BF16),
            vm((2, CUTS, 2 * q, wide), BF16),
            vm((2, CUTS, 2 * q, wide), F32),
            vm((2, CUTS, 2 * q, wide), BF16),
            vm((CUTS, q, wide), BF16),
            vm((CUTS, q, wide), BF16),
            vm((CUTS, q, wide), BF16),
            vm((CUTS, q, wide), BF16),
            vm((CUTS, q, wide), BF16),
            vm((CUTS, q, wide), BF16),
            vm((2, CUTS, rows, wide), BF16),
            vm((VISITS - 1, 8, lanes), F32),
            vm((VISITS - 1, 8, lanes), F32),
            vm((2, 8, lanes), F32),
            vm((2, 8, lanes), F32),
            pltpu.SemaphoreType.DMA((5 + 2 * CUTS,)),
            pltpu.SemaphoreType.DMA((3,)),
            pltpu.SemaphoreType.DMA((LEAVING,)),
            pltpu.SemaphoreType.DMA((TICKETS,)),
        ],
        compiler_params=pltpu.CompilerParams(
            collective_id=0, has_side_effects=True, vmem_limit_bytes=62 * 2**20
        ),
    )(xi, xt, wi, wt, scale, shift, partner)
    return pl.pallas_call(
        store,
        out_shape=(
            jax.ShapeDtypeStruct((rows, share), BF16),
            jax.ShapeDtypeStruct((rows, share), BF16),
            jax.ShapeDtypeStruct((rows,), F32),
        ),
        in_specs=[pl.BlockSpec(memory_space=pl.ANY)] * 3,
        out_specs=(pl.BlockSpec(memory_space=pl.ANY),) * 3,
        scratch_shapes=[vm((rows, share), BF16), vm((rows, share), BF16), vm((rows,), F32), pltpu.SemaphoreType.DMA((6,))],
        compiler_params=pltpu.CompilerParams(vmem_limit_bytes=62 * 2**20),
    )(gi, gt, loss)


def solution(mesh):
    placed = (P("dp", "mp"), P("dp", "mp"), P("mp", None), P("mp", None), P(), P(), P("dp", None))
    return jax.shard_map(
        functools.partial(shards, mesh.shape["dp"]),
        mesh=mesh,
        in_specs=placed,
        out_specs=(P("dp", "mp"), P("dp", "mp"), P("dp")),
        check_vma=False,
    )
```
